128 devices in a mesh: ep: 16 (over x, z), tp: 8 (over y, core).
Axes of the slice: x: 4, y: 4, z: 4, core: 2. Of those that a mesh axis runs over, the one named last changes fastest.
Arguments:
- tokens: bfloat16 [2, 2048, 4096], P(None, 'ep', 'tp'), may hold values from -6 to 6
- expert_ids: int32 [2, 2048, 8], P(None, 'ep'), may hold values from 0 to 63, all different within a row; in each aligned block of 128 rows (0 to 127, 128 to 255, ..., all dimensions but the last counted through in order) at most 20 rows name the same one
- route_weight: float32 [2, 2048, 8], P(None, 'ep'), may hold values from 0.1 to 1
- gate_weight: bfloat16 [64, 1536, 4096], P('ep', 'tp'), may hold values from -0.09375 to 0.09375
- up_weight: bfloat16 [64, 1536, 4096], P('ep', 'tp'), may hold values from -0.09375 to 0.09375
- down_weight: bfloat16 [64, 1536, 4096], P('ep', None, 'tp'), may hold values from -0.15625 to 0.15625
- home_slot: int32 [64], replicated, may hold values from 0 to 63, as said below
- spare_expert: int32 [16], replicated, may hold values from 0 to 63, as said below
Outputs:
- mixed: bfloat16 [2, 2048, 4096], P(None, 'ep', 'tp')
- spare_gate: bfloat16 [16, 1536, 4096], P('ep', 'tp')
- spare_up: bfloat16 [16, 1536, 4096], P('ep', 'tp')
- spare_down: bfloat16 [16, 1536, 4096], P('ep', None, 'tp')
The draws below stay inside these ranges and needn't reach their ends.
Inputs may be any that keep to these rules, and one draw needn't show every extreme that they name: `home_slot`: a permutation; slot s belongs to ep index s // 4. `spare_expert`: names at most 6 distinct experts, whose home slots lie on distinct ep indices; entry d never names an expert whose home slot lies on ep index d. `expert_ids`: each token names 8 distinct experts; in each micro-step the 128 tokens of one ep index name one expert at most 20 times.
All inputs are finite; a program needn't handle non-finite values.
Results may differ from the reference program's by a relative error of at most 0.0058.
Values may be sent and summed in bfloat16 or wider, within the bound.
A program may use at most 192 MiB of HBM per device.

```python
import math
import jax
import jax.numpy as jnp
import numpy as np
from jax import lax

D = 4096
FF = 1536
TOP = 8
EXP_DEV = 4
HOT = 6
STEPS = 2
TOK_EP = 128
EXPERTS = 64
TOKENS = 2048
CAP = 20
N_EP = 16


def swap_into(slot_owner, slot_index, expert_id):
    current = jnp.argmax((slot_owner == expert_id).astype(jnp.int32)).astype(jnp.int32)
    displaced = slot_owner[slot_index]
    slot_owner = slot_owner.at[current].set(displaced)
    return slot_owner.at[slot_index].set(expert_id)


def layout(key):
    base_key = jax.random.fold_in(key, 7)
    key_perm, key_device, key_local = jax.random.split(base_key, 3)
    slot_owner = jax.random.permutation(key_perm, EXPERTS).astype(jnp.int32)
    hot_device = jax.random.permutation(key_device, N_EP)[:HOT].astype(jnp.int32)
    hot_local = jax.random.randint(key_local, (HOT,), 0, EXP_DEV).astype(jnp.int32)
    hot_slot = (hot_device * EXP_DEV + hot_local).astype(jnp.int32)
    slot_owner = swap_into(slot_owner, hot_slot[0], jnp.int32(EXPERTS - 1))
    slot_owner = swap_into(slot_owner, hot_slot[1], jnp.int32(0))
    slot_iota = jnp.arange(EXPERTS, dtype=jnp.int32)
    home_table = jnp.zeros((EXPERTS,), jnp.int32).at[slot_owner].set(slot_iota)
    hot_expert = slot_owner[hot_slot]
    device_iota = jnp.arange(N_EP, dtype=jnp.int32)
    chosen = device_iota % HOT
    chosen = jnp.where(hot_device[chosen] == device_iota, (chosen + 1) % HOT, chosen)
    return (home_table, hot_expert[chosen].astype(jnp.int32))


def draw_home_slot(key, part):
    return layout(key)[0]


def draw_spare_expert(key, part):
    return layout(key)[1]


def block_scale(rng, extent, pieces, low, largest):
    gain, own = 1.0, jax.random.fold_in(rng, 6)
    for dim, blocks in pieces:
        heights = jnp.exp(jax.random.uniform(jax.random.fold_in(own, dim), (blocks,), jnp.float32, low / len(pieces), largest / len(pieces)))
        gain = gain * jnp.repeat(heights, extent[dim] // blocks).reshape([-1 if axis == dim else 1 for axis in range(len(extent))])
    return gain


def deal_out(rng, own, number, rows, number_of, top, limit, lean):
    order = jax.random.permutation(rng, number_of)
    packed, usual = shares(number_of, rows * top, limit, lean, True), shares(number_of, rows * top, limit, lean, False)
    places = jnp.arange(number_of)

    def named(sizes, offset_by):
        used = int((sizes > 0).sum())
        fixed = max(1, used // 4)
        passed = fixed + (places - fixed + offset_by * (used - fixed)) % max(1, number_of - fixed)
        return jnp.zeros((number_of,), jnp.int32).at[order[jnp.where(places < fixed, places, passed)]].set(jnp.asarray(sizes, jnp.int32))

    sizes = jnp.where(number % 4 == 0, named(packed, number // 4), named(usual, number - number // 4 - 1))
    mixed = jax.random.permutation(jax.random.fold_in(own, 3), number_of)
    source_of, taker = mixed[0:number_of // 2 * 2:2], mixed[1:number_of // 2 * 2:2]
    margin = jnp.minimum(sizes[source_of] - 1, limit - sizes[taker]) // 2
    margin = jnp.where((source_of == order[0]) | (taker == order[0]) | (sizes[taker] == 0), 0, jnp.maximum(margin, 0))
    passed = jax.random.randint(jax.random.fold_in(own, 4), (number_of // 2,), 0, 1 << 20) % (margin + 1)
    sizes = sizes.at[source_of].add(-passed).at[taker].add(passed)
    labels = jnp.searchsorted(jnp.cumsum(sizes), jnp.arange(rows * top), side="right").astype(jnp.int32)
    grid = labels.reshape(top, rows).T
    grid = grid[jax.random.permutation(jax.random.fold_in(own, 1), rows)]
    offset_by = jax.random.randint(jax.random.fold_in(own, 2), (rows, 1), 0, top)
    return jnp.take_along_axis(grid, (jnp.arange(top)[None, :] + offset_by) % top, axis=1)


def shares(count, total, limit, lean, full):
    weights = [(1 << 20) // math.isqrt(standing ** lean) + 1 for standing in range(1, count + 1)]
    largest = limit if full else min(limit, max(-(-total // count), total * weights[0] // sum(weights)))
    least = 1 if total - largest >= count - 1 else 0
    given, spare = [largest] + [least] * (count - 1), total - largest - least * (count - 1)
    while spare > 0:
        candidates = [i for i in range(1, count) if given[i] < largest] or [i for i in range(1, count) if given[i] < limit]
        whole, remaining = sum([weights[i] for i in candidates]), spare
        for i in candidates:
            more = min(limit - given[i], max(1, remaining * weights[i] // whole), spare)
            given[i] = given[i] + more
            spare = spare - more
    return np.array(given)


def normal_values(own_key, dims, width, bound, cuts=(), kind=jnp.bfloat16):
    gain = block_scale(own_key, dims, cuts, -0.22, 0.18) if cuts else 1.0
    result = jax.random.normal(own_key, dims, jnp.float32) * width * gain
    return jnp.minimum(jnp.maximum(result, -bound), bound).astype(kind)


def setup_inputs(seed: int = 0) -> dict:
    streams_of = jax.random.split(jax.random.key(seed), 9)
    tokens = normal_values(streams_of[0], (STEPS, TOKENS, D), 1.0, 6.0, ((1, 16), (2, 8)))
    expert_ids_keys = jax.random.split(jax.random.fold_in(streams_of[1], 1), STEPS * TOKENS // TOK_EP)
    expert_ids_turns = jax.random.permutation(jax.random.fold_in(streams_of[1], 3), STEPS * TOKENS // TOK_EP)
    expert_ids = jax.vmap(lambda own, number: deal_out(jax.random.fold_in(streams_of[1], 2), own, number, TOK_EP, EXPERTS, TOP, CAP, 1))(expert_ids_keys, expert_ids_turns).reshape((STEPS, TOKENS, TOP))
    route_weight = jnp.clip(jnp.exp(math.log(1.0) - 2.3025851 * jax.random.uniform(streams_of[2], (STEPS, TOKENS, TOP), jnp.float32) ** block_scale(streams_of[2], (STEPS, TOKENS, TOP), ((1, 16),), -0.2, 0.2)), 0.1, 1.0)
    gate_weight = normal_values(streams_of[3], (EXPERTS, FF, D), D ** -0.5, 0.09375, ((0, 16), (1, 8)))
    up_weight = normal_values(streams_of[4], (EXPERTS, FF, D), D ** -0.5, 0.09375, ((0, 16), (1, 8)))
    down_weight = normal_values(streams_of[5], (EXPERTS, FF, D), FF ** -0.5, 0.15625, ((0, 16), (2, 8)))
    home_slot = draw_home_slot(jax.random.fold_in(streams_of[8], 71), 0)
    spare_expert = draw_spare_expert(jax.random.fold_in(streams_of[8], 71), 0)
    return {"tokens": tokens, "expert_ids": expert_ids, "route_weight": route_weight, "gate_weight": gate_weight, "up_weight": up_weight, "down_weight": down_weight, "home_slot": home_slot, "spare_expert": spare_expert}


def reference(tokens, expert_ids, route_weight, gate_weight, up_weight, down_weight, home_slot, spare_expert):
    flat_tokens = tokens.reshape(STEPS * TOKENS, D)
    pair_slot = home_slot[expert_ids.reshape(-1)].astype(jnp.int32)
    pair_weight = route_weight.reshape(-1)
    pair_owner = jnp.arange(STEPS * TOKENS * TOP, dtype=jnp.int32) // TOP
    row_limit = min(CAP * STEPS * N_EP, STEPS * TOKENS * TOP)

    def one_slot(running, slot_id):
        matched = pair_slot == slot_id
        ordering = jnp.argsort(jnp.where(matched, 0, 1).astype(jnp.int32), stable=True)[:row_limit]
        valid = matched[ordering]
        owners = pair_owner[ordering]
        picked = flat_tokens[owners]
        gate_proj = jnp.dot(picked, gate_weight[slot_id].T, preferred_element_type=jnp.float32)
        up_proj = jnp.dot(picked, up_weight[slot_id].T, preferred_element_type=jnp.float32)
        hidden = (jax.nn.silu(gate_proj) * up_proj).astype(jnp.bfloat16)
        expert_out = jnp.dot(hidden, down_weight[slot_id], preferred_element_type=jnp.float32).astype(jnp.bfloat16)
        scale = jnp.where(valid, pair_weight[ordering], jnp.float32(0.0))
        running = running.at[owners].add(expert_out.astype(jnp.float32) * scale[:, None])
        return running, None

    running, unused = lax.scan(one_slot, jnp.zeros((STEPS * TOKENS, D), jnp.float32), jnp.arange(EXPERTS, dtype=jnp.int32))
    mixed = running.reshape(STEPS, TOKENS, D).astype(jnp.bfloat16)
    spare_slot = home_slot[spare_expert].astype(jnp.int32)
    return mixed, gate_weight[spare_slot], up_weight[spare_slot], down_weight[spare_slot]
```

```python
import functools

import jax
import jax.numpy as jnp
import numpy as np
from jax import lax
from jax.experimental import pallas as pl
from jax.experimental.pallas import tpu as pltpu
from jax.sharding import PartitionSpec as P

MESH = pl.DeviceIdType.MESH
BF16 = jnp.bfloat16
F32 = jnp.float32
STEPS = 2
SIDE = 4
CAP = 20
SLOTS = 64
TOK = 128
BLOCK = 4 * CAP
ROWS = 16 * CAP
PIECE = 288
ANY = pl.BlockSpec(memory_space=pl.ANY)
VM = pl.BlockSpec(memory_space=pltpu.VMEM)
SM = pl.BlockSpec(memory_space=pltpu.SMEM)


def dot(a, b):
    return jnp.dot(a, b, preferred_element_type=F32)


def dot_t(a, b):
    return lax.dot_general(a, b, (((1,), (1,)), ((), ())), preferred_element_type=F32)


def iota(shape, dim):
    return lax.broadcasted_iota(jnp.int32, shape, dim)


def pack_kernel(own_ref, ids_ref, home_ref, tok_ref, wg, wu, wd, out_ref, pieces, sem):
    own = own_ref[0]

    def copies(j):
        h, p = j // 16, lax.rem(j, 16)
        px, pz = p // 4, lax.rem(p, 4)
        columns = pl.ds(pl.multiple_of(p * 256, 256), 256)
        rows = pl.ds(pl.multiple_of(h * 96, 16), 96)
        low = pl.ds(pl.multiple_of(h * 768 + p * 48, 16), 48)
        to = pieces.at[h, px, pz]
        return [
            pltpu.make_async_copy(wg.at[own, rows, columns], to.at[pl.ds(0, 96)], sem.at[j, 0]),
            pltpu.make_async_copy(wu.at[own, rows, columns], to.at[pl.ds(96, 96)], sem.at[j, 1]),
            pltpu.make_async_copy(wd.at[own, low, pl.ds(0, 256)], to.at[pl.ds(192, 48)], sem.at[j, 2]),
            pltpu.make_async_copy(wd.at[own, low, pl.ds(256, 256)], to.at[pl.ds(240, 48)], sem.at[j, 3]),
        ]

    def start(j, _):
        for c in copies(j):
            c.start()
        return 0

    lax.fori_loop(0, 32, start, 0)
    perm = (home_ref[...] == iota((SLOTS, SLOTS), 0)).astype(BF16)
    before = (iota((TOK, TOK), 0) < iota((TOK, TOK), 1)).astype(BF16)
    for s in range(STEPS):
        named = iota((SLOTS, TOK), 0)
        picked = jnp.zeros((SLOTS, TOK), F32)
        for k in range(8):
            picked = jnp.where(ids_ref[s, k : k + 1, :] == named, 1.0, picked)
        by_slot = dot(perm, picked.astype(BF16))
        position = dot(by_slot.astype(BF16), before)
        value = jnp.where(by_slot > 0.5, position, -1.0).astype(BF16)
        for x in range(SIDE):
            row = iota((ROWS, SLOTS), 0) + x * ROWS
            low = iota((ROWS, SLOTS), 1) * CAP
            spread = jnp.where((row >= low) & (row < low + CAP), 1.0, 0.0).astype(BF16)
            row = iota((ROWS, TOK), 0) + x * ROWS
            within = (row - ((row * 3277) >> 16) * CAP).astype(F32)
            placing = jnp.where(dot(spread, value) == within, 1.0, 0.0).astype(BF16)
            for h in range(2):
                block = dot(placing, tok_ref[s, :, h * 256 : (h + 1) * 256]).astype(BF16)
                out_ref[s, h, x] = block.reshape(SIDE, BLOCK, 256)

    def finish(j, _):
        for c in copies(j):
            c.wait()
        return 0

    lax.fori_loop(0, 32, finish, 0)


def mix_kernel(ids_ref, rw_ref, home_ref, back_ref, pieces, mixed_ref, gate, up, down, sem):
    def copies(j):
        h, p = j // 16, lax.rem(j, 16)
        px, pz = p // 4, lax.rem(p, 4)
        columns = pl.ds(pl.multiple_of(p * 256, 256), 256)
        rows = pl.ds(pl.multiple_of(h * 96, 16), 96)
        low = pl.ds(pl.multiple_of(h * 768 + p * 48, 16), 48)
        of = pieces.at[h, px, pz]
        return [
            pltpu.make_async_copy(of.at[pl.ds(0, 96)], gate.at[0, rows, columns], sem.at[j, 0]),
            pltpu.make_async_copy(of.at[pl.ds(96, 96)], up.at[0, rows, columns], sem.at[j, 1]),
            pltpu.make_async_copy(of.at[pl.ds(192, 48)], down.at[0, low, pl.ds(0, 256)], sem.at[j, 2]),
            pltpu.make_async_copy(of.at[pl.ds(240, 48)], down.at[0, low, pl.ds(256, 256)], sem.at[j, 3]),
        ]

    def start(j, _):
        for c in copies(j):
            c.start()
        return 0

    lax.fori_loop(0, 32, start, 0)
    perm = (home_ref[...] == iota((SLOTS, SLOTS), 1)).astype(BF16)
    before = (iota((TOK, TOK), 1) < iota((TOK, TOK), 0)).astype(BF16)
    for s in range(STEPS):
        named = iota((TOK, SLOTS), 1)
        picked = jnp.zeros((TOK, SLOTS), F32)
        scale = jnp.zeros((TOK, SLOTS), F32)
        for k in range(8):
            match = ids_ref[s, :, k : k + 1] == named
            picked = jnp.where(match, 1.0, picked)
            scale = jnp.where(match, rw_ref[s, :, k : k + 1], scale)
        by_slot = dot(picked.astype(BF16), perm)
        position = dot(before, by_slot.astype(BF16))
        value = jnp.where(by_slot > 0.5, position, -1.0).astype(BF16)
        high = scale.astype(BF16)
        rest = (scale - high.astype(F32)).astype(BF16)
        high = dot(high, perm).astype(BF16)
        rest = dot(rest, perm).astype(BF16)
        totals = [jnp.zeros((TOK, 256), F32)] * 2
        for x in range(SIDE):
            row = iota((SLOTS, ROWS), 1) + x * ROWS
            low = iota((SLOTS, ROWS), 0) * CAP
            spread = jnp.where((row >= low) & (row < low + CAP), 1.0, 0.0).astype(BF16)
            row = iota((TOK, ROWS), 1) + x * ROWS
            within = (row - ((row * 3277) >> 16) * CAP).astype(F32)
            here = dot(value, spread) == within
            high_row = jnp.where(here, dot(high, spread), 0.0).astype(BF16)
            rest_row = jnp.where(here, dot(rest, spread), 0.0).astype(BF16)
            for h in range(2):
                block = back_ref[s, h, x].reshape(ROWS, 256)
                totals[h] = totals[h] + dot(high_row, block) + dot(rest_row, block)
        for h in range(2):
            mixed_ref[s, :, h * 256 : (h + 1) * 256] = totals[h].astype(BF16)

    def finish(j, _):
        for c in copies(j):
            c.wait()
        return 0

    lax.fori_loop(0, 32, finish, 0)


class Exchange:
    def __init__(self, number, src, mid, dst, send, recv):
        ep, tp = lax.axis_index("ep"), lax.axis_index("tp")
        self.ex, self.ez, self.tp = ep // SIDE, lax.rem(ep, SIDE), tp
        self.src, self.mid, self.dst = src, mid, dst
        self.send, self.recv, self.number = send, recv, number
        self.started = []

    def copy(self, phase, half, d):
        ex, ez = self.ex, self.ez
        along_x = half == phase
        x = lax.rem(ex + d, SIDE) if along_x else ex
        z = ez if along_x else lax.rem(ez + d, SIDE)
        if phase == 0:
            a = self.src.at[0, x] if half == 0 else self.src.at[1, :, z]
            b = self.mid.at[half, ex if half == 0 else ez]
        else:
            a = self.mid.at[half, :, z if half == 0 else x]
            b = self.dst.at[0, :, ez] if half == 0 else self.dst.at[1, ex]
        send = self.send.at[self.number, phase, half, d]
        if d == 0:
            return pltpu.make_async_copy(a, b, send)
        recv = self.recv.at[self.number, phase, half, d]
        return pltpu.make_async_remote_copy(
            a, b, send, recv, device_id=(x * SIDE + z, self.tp), device_id_type=MESH
        )

    def start(self, phase):
        for d in (2, 1, 3, 0):
            for half in range(2):
                c = self.copy(phase, half, d)
                c.start()
                self.started.append((phase, d, c))

    def arrive(self, phase):
        for at, d, c in self.started:
            if at == phase:
                c.wait() if d == 0 else c.wait_recv()

    def forward(self):
        self.arrive(0)
        self.start(1)

    def sent(self):
        for _, d, c in self.started:
            if d:
                c.wait_send()


class Ring:
    def __init__(self, number, ref, width, send, recv):
        self.ep, self.tp = lax.axis_index("ep"), lax.axis_index("tp")
        self.y = self.tp // 2
        self.ref, self.width, self.number = ref, width, number
        self.send, self.recv = send, recv
        self.all = {}

    def copy(self, kind):
        y = lax.rem(self.y + (0, 0, 3, 1)[kind], 4)
        to = lax.rem(self.tp + (2, 6, 2, 6)[kind], 8)
        rows = (pl.ds(0, ROWS), pl.ds(0, ROWS), pl.ds(0, ROWS // 2), pl.ds(ROWS // 2, ROWS // 2))[kind]
        part = self.ref.at[rows, pl.ds(pl.multiple_of(y * self.width, 128), self.width)]
        return pltpu.make_async_remote_copy(
            part,
            part,
            self.send.at[self.number, kind],
            self.recv.at[self.number, kind],
            device_id=(self.ep, to),
            device_id_type=MESH,
        )

    def start(self):
        for kind in (0, 1):
            self.all[kind] = self.copy(kind)
            self.all[kind].start()

    def forward(self):
        for kind in (0, 1):
            self.all[kind].wait_recv()
            self.all[kind + 2] = self.copy(kind + 2)
            self.all[kind + 2].start()

    def arrive(self):
        for kind in (2, 3):
            self.all[kind].wait_recv()

    def sent(self):
        for c in self.all.values():
            c.wait_send()


def main_kernel(
    sel, perm, outgoing, pieces, wg, wu, wd,
    returned, landed, mid_a, mid_b, mid_r,
    gate_w, up_w, down_w, xs, hs, swap, outs, arrived, results, mid_d, spread, chosen, acc,
    a_send, a_recv, x_send, x_recv, h_send, h_recv, c_send, c_recv, w_send, w_recv, w_local,
):
    ep, tp = lax.axis_index("ep"), lax.axis_index("tp")
    ex, ez = ep // SIDE, lax.rem(ep, SIDE)
    core = lax.rem(tp, 2)
    mate = (ep, tp + 1 - 2 * core)

    barrier = pltpu.get_barrier_semaphore()
    for d in range(1, SIDE):
        pl.semaphore_signal(barrier, inc=1, device_id=(lax.rem(ex + d, SIDE) * SIDE + ez, tp), device_id_type=MESH)
        pl.semaphore_signal(barrier, inc=1, device_id=(ex * SIDE + lax.rem(ez + d, SIDE), tp), device_id_type=MESH)
    pl.semaphore_signal(barrier, inc=1, device_id=(ep, lax.rem(tp + 2, 8)), device_id_type=MESH)
    pl.semaphore_signal(barrier, inc=1, device_id=(ep, lax.rem(tp + 6, 8)), device_id_type=MESH)
    pl.semaphore_signal(barrier, inc=1, device_id=mate, device_id_type=MESH)
    pl.semaphore_wait(barrier, 9)

    deal = [Exchange(s, outgoing.at[s], mid_d.at[s], arrived.at[s], a_send, a_recv) for s in range(STEPS)]
    give = [Exchange(2 + s, results.at[s], mid_r.at[s], returned.at[s], a_send, a_recv) for s in range(STEPS)]
    scatter = Exchange(4, pieces, mid_a, spread, a_send, a_recv)
    gather = Exchange(5, chosen, mid_b, landed, a_send, a_recv)
    x_ring = [Ring(q, xs.at[q // 2, q % 2], 1024, x_send, x_recv) for q in range(4)]
    h_ring = [Ring(q, hs.at[q // 2, q % 2], 384, h_send, h_recv) for q in range(4)]

    deal[0].start(0)
    deal[1].start(0)

    own_two, mate_two = pl.ds(2 * core, 2), pl.ds(2 - 2 * core, 2)
    own_rows = pl.ds(pl.multiple_of(core * 192, 16), 192)
    own_half = pl.ds(pl.multiple_of(core * 512, 512), 512)
    mate_half = pl.ds(pl.multiple_of(512 - core * 512, 512), 512)
    weights = []
    for n, (w, held) in enumerate(((wg, gate_w), (wu, up_w), (wd, down_w))):
        to = held.at[:, :, own_half] if n == 2 else held.at[:, own_rows]
        mine = pltpu.make_async_copy(w.at[own_two], to, w_local.at[n])
        theirs = pltpu.make_async_remote_copy(
            w.at[mate_two], to, w_send.at[n], w_recv.at[n], device_id=mate, device_id_type=MESH
        )
        mine.start()
        theirs.start()
        weights.append((mine, theirs))

    own_perm = pl.ds(pl.multiple_of(core * 160, 16), 160)
    mate_perm = pl.ds(pl.multiple_of(160 - core * 160, 16), 160)

    def regroup(s):
        def one(g, _):
            rows = pl.ds(pl.multiple_of(g * BLOCK, 16), BLOCK)
            for h in range(2):
                block = arrived[s, h, g].reshape(ROWS, 256)
                mine = dot(perm[own_perm, :], block).astype(BF16)
                theirs = dot(perm[mate_perm, :], block).astype(BF16)
                columns = pl.ds(pl.multiple_of(tp * 512 + h * 256, 256), 256)
                for i in range(2):
                    xs[s, i, rows, columns] = mine[i * BLOCK : (i + 1) * BLOCK]
                    swap[s, i, rows, pl.ds(h * 256, 256)] = theirs[i * BLOCK : (i + 1) * BLOCK]
            return 0

        lax.fori_loop(0, SIDE, one, 0)
        c = pltpu.make_async_remote_copy(
            swap.at[s],
            xs.at[s, :, :, pl.ds(pl.multiple_of(tp * 512, 512), 512)],
            c_send.at[s],
            c_recv.at[s],
            device_id=mate,
            device_id_type=MESH,
        )
        c.start()
        return c

    def hidden(q):
        s, i = q // 2, q % 2
        acc[...] = jnp.zeros_like(acc)

        def one(k, _):
            columns = pl.ds(pl.multiple_of(k * 512, 512), 512)
            block = xs[s, i, :, columns]
            acc[0] += dot_t(block, gate_w[i, :, columns])
            acc[1] += dot_t(block, up_w[i, :, columns])
            return 0

        lax.fori_loop(0, 8, one, 0)
        columns = pl.ds(pl.multiple_of((tp // 2) * 384, 128), 384)
        gate = acc[0]
        hs[s, i, :, columns] = (gate / (1.0 + jnp.exp(-gate)) * acc[1]).astype(BF16)
        h_ring[q].start()

    def out(q):
        s, i = q // 2, q % 2

        def one(n, _):
            columns = pl.ds(pl.multiple_of(n * 256, 256), 256)
            mine = pl.ds(pl.multiple_of(core * 512 + n * 256, 256), 256)
            theirs = pl.ds(pl.multiple_of(512 - core * 512 + n * 256, 256), 256)
            block = hs[s, i]
            swap[s, i, :, columns] = dot(block, down_w[i, :, theirs]).astype(BF16)
            outs[s, 2 * core + i, :, columns] = dot(block, down_w[i, :, mine]).astype(BF16)
            return 0

        lax.fori_loop(0, 2, one, 0)
        c = pltpu.make_async_remote_copy(
            swap.at[s, i],
            outs.at[s, 2 * core + i],
            c_send.at[2 + q],
            c_recv.at[2 + q],
            device_id=mate,
            device_id_type=MESH,
        )
        c.start()
        return c

    def ungroup(s):
        def one(g, _):
            rows = pl.ds(pl.multiple_of(g * BLOCK, 16), BLOCK)
            for h in range(2):
                block = outs[s, :, rows, pl.ds(h * 256, 256)].reshape(ROWS, 256)
                results[s, h, g] = dot(perm[...], block).astype(BF16).reshape(SIDE, BLOCK, 256)
            return 0

        lax.fori_loop(0, SIDE, one, 0)
        give[s].start(0)

    def choose():
        def one(d, _):
            x, z = d // SIDE, lax.rem(d, SIDE)
            home = sel[d]
            for h in range(2):
                chosen[h, x, z] = spread[h, home // SIDE, lax.rem(home, SIDE)]
            return 0

        lax.fori_loop(0, 16, one, 0)
        gather.start(0)

    deal[0].forward()
    deal[1].forward()
    scatter.start(0)
    deal[0].arrive(1)
    swap_x = [regroup(0)]
    swap_x[0].wait()
    x_ring[0].start()
    deal[1].arrive(1)
    swap_x.append(regroup(1))
    swap_x[1].wait()
    x_ring[0].forward()
    x_ring[1].start()
    scatter.forward()
    for mine, theirs in weights:
        mine.wait()
        theirs.wait_recv()
    x_ring[0].arrive()
    hidden(0)
    x_ring[1].forward()
    x_ring[2].start()
    h_ring[0].forward()
    x_ring[1].arrive()
    hidden(1)
    scatter.arrive(1)
    choose()
    x_ring[2].forward()
    x_ring[3].start()
    h_ring[0].arrive()
    swap_o = [out(0)]
    h_ring[1].forward()
    x_ring[2].arrive()
    hidden(2)
    h_ring[1].arrive()
    swap_o.append(out(1))
    swap_o[0].wait()
    swap_o[1].wait()
    ungroup(0)
    x_ring[3].forward()
    gather.forward()
    h_ring[2].forward()
    x_ring[3].arrive()
    hidden(3)
    give[0].forward()
    h_ring[2].arrive()
    swap_o.append(out(2))
    h_ring[3].forward()
    h_ring[3].arrive()
    swap_o.append(out(3))
    swap_o[2].wait()
    swap_o[3].wait()
    ungroup(1)
    give[1].forward()
    gather.arrive(1)
    give[0].arrive(1)
    give[1].arrive(1)
    for one in (*deal, *give, scatter, gather, *x_ring, *h_ring):
        one.sent()
    for _, theirs in weights:
        theirs.wait_send()


def permutation():
    index = np.arange(ROWS).reshape(SIDE, SIDE, CAP).transpose(1, 0, 2).reshape(-1)
    return np.eye(ROWS, dtype=np.float32)[index]


def shards(tokens, expert_ids, route_weight, gate_weight, up_weight, down_weight, home_slot, spare_expert):
    own_index = lax.axis_index("ep")
    experts = lax.iota(jnp.int32, SLOTS)
    spare_slot = jnp.sum(jnp.where(spare_expert[:, None] == experts, home_slot, 0), axis=1)
    spare_home = spare_slot // 4
    own_slot = jnp.max(jnp.where(spare_home == own_index, spare_slot % 4, 0)).reshape(1)
    piece_shape = jax.ShapeDtypeStruct((2, SIDE, SIDE, PIECE, 256), BF16)
    row_shape = jax.ShapeDtypeStruct((STEPS, 2, SIDE, SIDE, BLOCK, 256), BF16)

    outgoing, pieces = pl.pallas_call(
        pack_kernel,
        out_shape=(row_shape, piece_shape),
        in_specs=[SM, VM, VM, VM, ANY, ANY, ANY],
        out_specs=(VM, ANY),
        scratch_shapes=[pltpu.SemaphoreType.DMA((32, 4))],
        compiler_params=pltpu.CompilerParams(vmem_limit_bytes=32 * 2**20),
        name="pack",
    )(own_slot, expert_ids.transpose(0, 2, 1), home_slot.reshape(1, SLOTS), tokens, gate_weight, up_weight, down_weight)

    returned, landed, *_ = pl.pallas_call(
        main_kernel,
        out_shape=(row_shape, piece_shape, piece_shape, piece_shape, row_shape),
        in_specs=[SM, VM, ANY, ANY, ANY, ANY, ANY],
        out_specs=(ANY,) * 5,
        scratch_shapes=[
            pltpu.VMEM((2, 384, 4096), BF16),
            pltpu.VMEM((2, 384, 4096), BF16),
            pltpu.VMEM((2, 1536, 1024), BF16),
            pltpu.VMEM((STEPS, 2, ROWS, 4096), BF16),
            pltpu.VMEM((STEPS, 2, ROWS, 1536), BF16),
            pltpu.VMEM((STEPS, 2, ROWS, 512), BF16),
            pltpu.VMEM((STEPS, 4, ROWS, 512), BF16),
            pltpu.VMEM(row_shape.shape, BF16),
            pltpu.VMEM(row_shape.shape, BF16),
            pltpu.VMEM(row_shape.shape, BF16),
            pltpu.VMEM(piece_shape.shape, BF16),
            pltpu.VMEM(piece_shape.shape, BF16),
            pltpu.VMEM((2, ROWS, 384), F32),
            pltpu.SemaphoreType.DMA((6, 2, 2, 4)),
            pltpu.SemaphoreType.DMA((6, 2, 2, 4)),
            pltpu.SemaphoreType.DMA((4, 4)),
            pltpu.SemaphoreType.DMA((4, 4)),
            pltpu.SemaphoreType.DMA((4, 4)),
            pltpu.SemaphoreType.DMA((4, 4)),
            pltpu.SemaphoreType.DMA((6,)),
            pltpu.SemaphoreType.DMA((6,)),
            pltpu.SemaphoreType.DMA((3,)),
            pltpu.SemaphoreType.DMA((3,)),
            pltpu.SemaphoreType.DMA((3,)),
        ],
        compiler_params=pltpu.CompilerParams(
            collective_id=0, has_side_effects=True, vmem_limit_bytes=60 * 2**20
        ),
        name="exchange",
    )(spare_home, jnp.asarray(permutation(), BF16), outgoing, pieces, gate_weight, up_weight, down_weight)

    return pl.pallas_call(
        mix_kernel,
        out_shape=(
            jax.ShapeDtypeStruct(tokens.shape, BF16),
            jax.ShapeDtypeStruct((1,) + gate_weight.shape[1:], BF16),
            jax.ShapeDtypeStruct((1,) + up_weight.shape[1:], BF16),
            jax.ShapeDtypeStruct((1,) + down_weight.shape[1:], BF16),
        ),
        in_specs=[VM, VM, VM, VM, ANY],
        out_specs=(VM, ANY, ANY, ANY),
        scratch_shapes=[pltpu.SemaphoreType.DMA((32, 4))],
        compiler_params=pltpu.CompilerParams(vmem_limit_bytes=32 * 2**20),
        name="mix",
    )(expert_ids, route_weight, home_slot.reshape(SLOTS, 1), returned, landed)


def solution(mesh):
    placed = (
        P(None, "ep", "tp"),
        P(None, "ep", None),
        P(None, "ep", None),
        P("ep", "tp", None),
        P("ep", "tp", None),
        P("ep", None, "tp"),
        P(),
        P(),
    )
    return jax.shard_map(
        shards,
        mesh=mesh,
        in_specs=placed,
        out_specs=(
            P(None, "ep", "tp"),
            P("ep", "tp", None),
            P("ep", "tp", None),
            P("ep", None, "tp"),
        ),
        check_vma=False,
    )
```

```python
import functools

import jax
import jax.numpy as jnp
import numpy as np
from jax import lax
from jax.experimental import pallas as pl
from jax.experimental.pallas import tpu as pltpu
from jax.sharding import PartitionSpec as P

MESH = pl.DeviceIdType.MESH
BF16 = jnp.bfloat16
F32 = jnp.float32
STEPS = 2
SIDE = 4
CAP = 20
SLOTS = 64
TOK = 128
BLOCK = 4 * CAP
ROWS = 16 * CAP
PAIR = 48
PIECE = 288
HBM = pl.BlockSpec(memory_space=pltpu.MemorySpace.HBM)
VM = pl.BlockSpec(memory_space=pltpu.VMEM)
SM = pl.BlockSpec(memory_space=pltpu.SMEM)


def dot(a, b):
    return jnp.dot(a, b, preferred_element_type=F32)


def dot_t(a, b):
    return lax.dot_general(a, b, (((1,), (1,)), ((), ())), preferred_element_type=F32)


def dot_0(a, b):
    return lax.dot_general(a, b, (((0,), (0,)), ((), ())), preferred_element_type=F32)


def iota(shape, dim):
    return lax.broadcasted_iota(jnp.int32, shape, dim)


def slot_places(ids, home):
    to_slot = (home == iota((SLOTS, SLOTS), 0)).astype(BF16)
    before = (iota((TOK, TOK), 0) < iota((TOK, TOK), 1)).astype(BF16)
    named = iota((SLOTS, TOK), 0)
    picked = jnp.zeros((SLOTS, TOK), F32)
    for k in range(8):
        picked = jnp.where(ids[k : k + 1, :] == named, 1.0, picked)
    by_slot = dot(to_slot, picked.astype(BF16))
    position = dot(by_slot.astype(BF16), before)
    return jnp.where(by_slot > 0.5, position, -1.0).astype(BF16), to_slot


def rows_of(x):
    row = iota((ROWS, SLOTS), 0) + x * ROWS
    low = iota((ROWS, SLOTS), 1) * CAP
    spread = jnp.where((row >= low) & (row < low + CAP), 1.0, 0.0).astype(BF16)
    row = iota((ROWS, TOK), 0) + x * ROWS
    return spread, (row - ((row * 3277) >> 16) * CAP).astype(F32)


def pair_rows_of(x, i):
    def split(width):
        row = iota((SIDE * PAIR, width), 0)
        z = (row * 1366) >> 16
        rest = row - z * PAIR
        c = (rest * 3277) >> 16
        return z, rest, c

    z, rest, c = split(SLOTS)
    slot = (x * SIDE + z) * 4 + 2 * c + i
    spread = jnp.where((slot == iota((SIDE * PAIR, SLOTS), 1)) & (rest < 2 * CAP), 1.0, 0.0).astype(BF16)
    z, rest, c = split(TOK)
    return spread, jnp.where(rest < 2 * CAP, rest - c * CAP, -5).astype(F32)


def mix_kernel(
    ids_ref, rw_ref, home_ref, back_hbm, pair_hbm, pieces, mixed_ref, gate, up, down,
    back, back_pair, held, gate_v, up_v, down_v, in_sem, out_sem,
):
    loads = [pltpu.make_async_copy(pieces.at[h], held.at[h], in_sem.at[h]) for h in range(2)]
    loads.append(pltpu.make_async_copy(back_hbm, back, in_sem.at[2]))
    loads.append(pltpu.make_async_copy(pair_hbm, back_pair, in_sem.at[3]))
    for c in loads:
        c.start()
    writes = []
    for h in range(2):
        loads[h].wait()

        def one(p, _, h=h):
            of = held.at[h, p // SIDE, lax.rem(p, SIDE)]
            columns = pl.ds(pl.multiple_of(p * 256, 256), 256)
            low = pl.ds(pl.multiple_of(h * 768 + p * 48, 16), 48)
            gate_v[pl.ds(h * 96, 96), columns] = of[pl.ds(0, 96)]
            up_v[pl.ds(h * 96, 96), columns] = of[pl.ds(96, 96)]
            down_v[low, pl.ds(0, 256)] = of[pl.ds(192, 48)]
            down_v[low, pl.ds(256, 256)] = of[pl.ds(240, 48)]
            return 0

        lax.fori_loop(0, 16, one, 0)
        for n, (a, b, rows) in enumerate(((gate_v, gate, 96), (up_v, up, 96), (down_v, down, 768))):
            part = pl.ds(h * rows, rows)
            writes.append(pltpu.make_async_copy(a.at[part], b.at[0, part], out_sem.at[h, n]))
            writes[-1].start()
    loads[2].wait()
    loads[3].wait()
    for s in range(STEPS):
        places, to_slot = slot_places(ids_ref[s], home_ref[...])
        named = iota((SLOTS, TOK), 0)
        scale = jnp.zeros((SLOTS, TOK), F32)
        for k in range(8):
            scale = jnp.where(ids_ref[s, k : k + 1, :] == named, rw_ref[s, k : k + 1, :], scale)
        high = scale.astype(BF16)
        rest = (scale - high.astype(F32)).astype(BF16)
        high = dot(to_slot, high).astype(BF16)
        rest = dot(to_slot, rest).astype(BF16)
        totals = [jnp.zeros((TOK, 256), F32)] * 2
        parts = [(x, i) for x in range(SIDE) for i in range(2 if s else 1)]
        for x, i in parts:
            spread, within = pair_rows_of(x, i) if s else rows_of(x)
            here = dot(spread, places) == within
            high_row = jnp.where(here, dot(spread, high), 0.0).astype(BF16)
            rest_row = jnp.where(here, dot(spread, rest), 0.0).astype(BF16)
            for h in range(2):
                block = back_pair[i, h, x].reshape(SIDE * PAIR, 256) if s else back[h, x].reshape(ROWS, 256)
                totals[h] = totals[h] + dot_0(high_row, block) + dot_0(rest_row, block)
        for h in range(2):
            mixed_ref[s, :, h * 256 : (h + 1) * 256] = totals[h].astype(BF16)

    for c in writes:
        c.wait()


class Exchange:
    def __init__(self, number, src, mid, dst, send, recv):
        ep, tp = lax.axis_index("ep"), lax.axis_index("tp")
        self.ex, self.ez, self.tp = ep // SIDE, lax.rem(ep, SIDE), tp
        self.src, self.mid, self.dst = src, mid, dst
        self.send, self.recv, self.number = send, recv, number
        self.started = []

    def copy(self, phase, half, d):
        ex, ez = self.ex, self.ez
        along_x = half == phase
        x = lax.rem(ex + d, SIDE) if along_x else ex
        z = ez if along_x else lax.rem(ez + d, SIDE)
        if phase == 0:
            a = self.src.at[0, x] if half == 0 else self.src.at[1, :, z]
            b = self.mid.at[half, ex if half == 0 else ez]
        else:
            a = self.mid.at[half, :, z if half == 0 else x]
            b = self.dst.at[0, :, ez] if half == 0 else self.dst.at[1, ex]
        send = self.send.at[self.number, phase, half, d]
        if d == 0:
            return pltpu.make_async_copy(a, b, send)
        recv = self.recv.at[self.number, phase, half, d]
        return pltpu.make_async_remote_copy(
            a, b, send, recv, device_id=(x * SIDE + z, self.tp), device_id_type=MESH
        )

    def start(self, phase):
        for d in (2, 1, 3, 0):
            for half in range(2):
                c = self.copy(phase, half, d)
                c.start()
                self.started.append((phase, d, c))

    def arrive(self, phase):
        for at, d, c in self.started:
            if at == phase:
                c.wait() if d == 0 else c.wait_recv()

    def forward(self):
        self.arrive(0)
        self.start(1)

    def sent(self):
        for _, d, c in self.started:
            if d:
                c.wait_send()


class Ring:
    def __init__(self, number, ref, width, send, recv):
        self.ep, self.tp = lax.axis_index("ep"), lax.axis_index("tp")
        self.y = self.tp // 2
        self.ref, self.width, self.number = ref, width, number
        self.send, self.recv = send, recv
        self.all = {}

    def copy(self, kind):
        y = lax.rem(self.y + (0, 0, 3, 1)[kind], 4)
        to = lax.rem(self.tp + (2, 6, 2, 6)[kind], 8)
        rows = (pl.ds(0, ROWS), pl.ds(0, ROWS), pl.ds(0, ROWS // 2), pl.ds(ROWS // 2, ROWS // 2))[kind]
        part = self.ref.at[rows, pl.ds(pl.multiple_of(y * self.width, 128), self.width)]
        return pltpu.make_async_remote_copy(
            part,
            part,
            self.send.at[self.number, kind],
            self.recv.at[self.number, kind],
            device_id=(self.ep, to),
            device_id_type=MESH,
        )

    def start(self):
        for kind in (0, 1):
            self.all[kind] = self.copy(kind)
            self.all[kind].start()

    def forward(self):
        for kind in (0, 1):
            self.all[kind].wait_recv()
            self.all[kind + 2] = self.copy(kind + 2)
            self.all[kind + 2].start()

    def arrive(self):
        for kind in (2, 3):
            self.all[kind].wait_recv()

    def sent(self):
        for c in self.all.values():
            c.wait_send()


def main_kernel(
    home_s, spare_s, home_ref, ids_ref, tok_ref, perm, pair_perm, wg, wu, wd,
    returned, returned_pair, landed, mid_a,
    gate_w, up_w, down_w, xs, hs, swap, outs, arrived, outgoing, mid_d, mid_r, out_pair, mid_pair, spread, chosen, acc,
    a_send, a_recv, x_send, x_recv, h_send, h_recv, c_send, c_recv, w_send, w_recv, w_local, p_local, credit,
):
    ep, tp = lax.axis_index("ep"), lax.axis_index("tp")
    ex, ez = ep // SIDE, lax.rem(ep, SIDE)
    core = lax.rem(tp, 2)
    mate = (ep, tp + 1 - 2 * core)

    barrier = pltpu.get_barrier_semaphore()
    for d in range(1, SIDE):
        pl.semaphore_signal(barrier, inc=1, device_id=(lax.rem(ex + d, SIDE) * SIDE + ez, tp), device_id_type=MESH)
        pl.semaphore_signal(barrier, inc=1, device_id=(ex * SIDE + lax.rem(ez + d, SIDE), tp), device_id_type=MESH)
    pl.semaphore_signal(barrier, inc=1, device_id=(ep, lax.rem(tp + 2, 8)), device_id_type=MESH)
    pl.semaphore_signal(barrier, inc=1, device_id=(ep, lax.rem(tp + 6, 8)), device_id_type=MESH)
    pl.semaphore_signal(barrier, inc=1, device_id=mate, device_id_type=MESH)

    deal = [Exchange(s, outgoing.at[s], mid_d.at[s], arrived.at[s], a_send, a_recv) for s in range(STEPS)]
    give = [Exchange(2, outgoing.at[0], mid_r, returned, a_send, a_recv)]
    for i in range(2):
        give.append(Exchange(3 + i, out_pair.at[i], mid_pair.at[i], returned_pair.at[i], a_send, a_recv))
    scatter = Exchange(5, chosen, mid_a, spread, a_send, a_recv)
    gather = Exchange(6, chosen, spread, landed, a_send, a_recv)
    x_ring = [Ring(q, xs.at[q], 1024, x_send, x_recv) for q in range(4)]
    h_ring = [Ring(q, hs.at[q], 384, h_send, h_recv) for q in range(4)]

    own_two, mate_two = pl.ds(2 * core, 2), pl.ds(2 - 2 * core, 2)
    own_rows = pl.ds(pl.multiple_of(core * 192, 16), 192)
    own_half = pl.ds(pl.multiple_of(core * 512, 512), 512)
    mate_half = pl.ds(pl.multiple_of(512 - core * 512, 512), 512)
    weights = []
    for n, (w, held) in enumerate(((wg, gate_w), (wu, up_w), (wd, down_w))):
        to = held.at[:, :, own_half] if n == 2 else held.at[:, own_rows]
        mine = pltpu.make_async_copy(w.at[own_two], to, w_local.at[n])
        theirs = pltpu.make_async_remote_copy(
            w.at[mate_two], to, w_send.at[n], w_recv.at[n], device_id=mate, device_id_type=MESH
        )
        weights.append((mine, theirs))

    own_perm = pl.ds(pl.multiple_of(core * 160, 16), 160)
    mate_perm = pl.ds(pl.multiple_of(160 - core * 160, 16), 160)

    def regroup(s):
        def one(g, _):
            rows = pl.ds(pl.multiple_of(g * BLOCK, 16), BLOCK)
            for h in range(2):
                block = arrived[s, h, g].reshape(ROWS, 256)
                mine = dot(perm[own_perm, :], block).astype(BF16)
                theirs = dot(perm[mate_perm, :], block).astype(BF16)
                columns = pl.ds(pl.multiple_of(tp * 512 + h * 256, 256), 256)
                for i in range(2):
                    xs[2 * s + i, rows, columns] = mine[i * BLOCK : (i + 1) * BLOCK]
                    swap[s, i, rows, pl.ds(h * 256, 256)] = theirs[i * BLOCK : (i + 1) * BLOCK]
            return 0

        lax.fori_loop(0, SIDE, one, 0)
        c = pltpu.make_async_remote_copy(
            swap.at[s],
            xs.at[pl.ds(2 * s, 2), :, pl.ds(pl.multiple_of(tp * 512, 512), 512)],
            c_send.at[s],
            c_recv.at[s],
            device_id=mate,
            device_id_type=MESH,
        )
        c.start()
        return c

    def hidden(q):
        i = q % 2
        acc[...] = jnp.zeros_like(acc)

        def one(k, _):
            columns = pl.ds(pl.multiple_of(k * 512, 512), 512)
            block = xs[q, :, columns]
            acc[0] += dot_t(block, gate_w[i, :, columns])
            acc[1] += dot_t(block, up_w[i, :, columns])
            return 0

        lax.fori_loop(0, 8, one, 0)
        columns = pl.ds(pl.multiple_of((tp // 2) * 384, 128), 384)
        gate = acc[0]
        hs[q, :, columns] = (gate / (1.0 + jnp.exp(-gate)) * acc[1]).astype(BF16)
        h_ring[q].start()

    def out(q):
        s, i = q // 2, q % 2

        def one(n, _):
            columns = pl.ds(pl.multiple_of(n * 256, 256), 256)
            mine = pl.ds(pl.multiple_of(core * 512 + n * 256, 256), 256)
            theirs = pl.ds(pl.multiple_of(512 - core * 512 + n * 256, 256), 256)
            block = hs[q]
            swap[s, i, :, columns] = dot(block, down_w[i, :, theirs]).astype(BF16)
            outs[s, 2 * core + i, :, columns] = dot(block, down_w[i, :, mine]).astype(BF16)
            return 0

        lax.fori_loop(0, 2, one, 0)
        c = pltpu.make_async_remote_copy(
            swap.at[s, i],
            outs.at[s, 2 * core + i],
            c_send.at[2 + q],
            c_recv.at[2 + q],
            device_id=mate,
            device_id_type=MESH,
        )
        c.start()
        return c

    def ungroup():
        def one(g, _):
            rows = pl.ds(pl.multiple_of(g * BLOCK, 16), BLOCK)
            for h in range(2):
                block = outs[0, :, rows, pl.ds(h * 256, 256)].reshape(ROWS, 256)
                outgoing[0, h, g] = dot(perm[...], block).astype(BF16).reshape(SIDE, BLOCK, 256)
            return 0

        lax.fori_loop(0, SIDE, one, 0)
        give[0].start(0)

    def ungroup_pair(i):
        def one(g, _):
            rows = pl.ds(pl.multiple_of(g * BLOCK, 16), BLOCK)
            for h in range(2):
                columns = pl.ds(h * 256, 256)
                total = dot(pair_perm[0], outs[1, i, rows, columns]) + dot(pair_perm[1], outs[1, 2 + i, rows, columns])
                out_pair[i, h, g] = total.astype(BF16).reshape(SIDE, PAIR, 256)
            return 0

        lax.fori_loop(0, SIDE, one, 0)
        give[1 + i].start(0)

    def choose():
        def one(d, _):
            x, z = d // SIDE, lax.rem(d, SIDE)
            home = home_s[spare_s[d]] // 4
            for h in range(2):
                chosen[h, x, z] = spread[h, home // SIDE, lax.rem(home, SIDE)]
            return 0

        lax.fori_loop(0, 16, one, 0)
        for d in range(1, SIDE):
            along_x, along_z = lax.rem(ex + d, SIDE) * SIDE + ez, ex * SIDE + lax.rem(ez + d, SIDE)
            pl.semaphore_signal(credit, inc=1, device_id=(along_x, tp), device_id_type=MESH)
            pl.semaphore_signal(credit, inc=1, device_id=(along_z, tp), device_id_type=MESH)
        pl.semaphore_wait(credit, 6)
        gather.start(0)

    def place(s):
        places, _ = slot_places(ids_ref[s], home_ref[...])

        def one(x, _):
            spread_rows, within = rows_of(x)
            placing = jnp.where(dot(spread_rows, places) == within, 1.0, 0.0).astype(BF16)
            for h in range(2):
                block = dot(placing, tok_ref[s, :, h * 256 : (h + 1) * 256]).astype(BF16)
                outgoing[s, h, x] = block.reshape(SIDE, BLOCK, 256)
            return 0

        lax.fori_loop(0, SIDE, one, 0)

    def fetch(j):
        h, two, b = j // 8, lax.rem(j, 8), lax.rem(j, 3)
        rows = pl.ds(pl.multiple_of(h * 96, 16), 96)
        columns = pl.ds(pl.multiple_of(two * 512, 512), 512)
        low = pl.ds(pl.multiple_of(h * 768 + two * 96, 16), 96)
        to = pl.ds(pl.multiple_of(b * 96, 16), 96)
        return [
            pltpu.make_async_copy(wg.at[:, rows, columns], hs.at[:, to, pl.ds(0, 512)], p_local.at[b, 0]),
            pltpu.make_async_copy(wu.at[:, rows, columns], hs.at[:, to, pl.ds(512, 512)], p_local.at[b, 1]),
            pltpu.make_async_copy(wd.at[:, low, :], hs.at[:, to, pl.ds(1024, 512)], p_local.at[b, 2]),
        ]

    def fetch_start(j):
        for c in fetch(j):
            c.start()

    def cut():
        def find(d, own):
            slot = home_s[spare_s[d]]
            return jnp.maximum(own, jnp.where(slot // 4 == ep, lax.rem(slot, 4), 0))

        own = lax.fori_loop(0, 16, find, jnp.int32(0))

        def one(j, _):
            for c in fetch(j):
                c.wait()
            h, two, b = j // 8, lax.rem(j, 8), lax.rem(j, 3)
            px, pair = two // 2, lax.rem(two, 2)

            def pick(low, rows, columns):
                at = pl.ds(pl.multiple_of(b * 96 + low, 16), rows)
                value = hs[0, at, columns]
                for k in range(1, 4):
                    value = jnp.where(own == k, hs[k, at, columns], value)
                return value

            for z in range(2):
                to = chosen.at[h, px, 2 * pair + z]
                for n in range(2):
                    to[pl.ds(96 * n, 96)] = pick(0, 96, pl.ds(512 * n + 256 * z, 256))
                    to[pl.ds(192 + 48 * n, 48)] = pick(48 * z, 48, pl.ds(1024 + 256 * n, 256))
            return 0

        def more(j, _):
            one(j, 0)
            fetch_start(j + 3)
            return 0

        lax.fori_loop(0, 13, more, 0)
        lax.fori_loop(13, 16, one, 0)

    for j in range(3):
        fetch_start(j)
    place(0)
    pl.semaphore_wait(barrier, 9)
    deal[0].start(0)
    for mine, theirs in weights:
        theirs.start()
        mine.start()
    deal[0].forward()
    place(1)
    deal[0].arrive(1)
    swap_x = [regroup(0)]
    deal[1].start(0)
    swap_x[0].wait()
    x_ring[0].start()
    cut()
    deal[1].forward()
    scatter.start(0)
    x_ring[0].forward()
    x_ring[1].start()
    for mine, theirs in weights:
        mine.wait()
        theirs.wait_recv()
    x_ring[0].arrive()
    hidden(0)
    deal[1].arrive(1)
    swap_x.append(regroup(1))
    swap_x[1].wait()
    x_ring[1].forward()
    x_ring[2].start()
    h_ring[0].forward()
    scatter.forward()
    x_ring[1].arrive()
    hidden(1)
    h_ring[0].arrive()
    swap_o = [out(0)]
    x_ring[2].forward()
    x_ring[3].start()
    h_ring[1].forward()
    scatter.arrive(1)
    scatter.sent()
    choose()
    x_ring[2].arrive()
    hidden(2)
    h_ring[1].arrive()
    swap_o.append(out(1))
    swap_o[0].wait()
    swap_o[1].wait()
    for one in deal:
        one.sent()
    ungroup()
    x_ring[3].forward()
    h_ring[2].forward()
    gather.forward()
    x_ring[3].arrive()
    hidden(3)
    give[0].forward()
    h_ring[2].arrive()
    swap_o.append(out(2))
    swap_o[2].wait()
    ungroup_pair(0)
    h_ring[3].forward()
    h_ring[3].arrive()
    swap_o.append(out(3))
    swap_o[3].wait()
    ungroup_pair(1)
    give[1].forward()
    give[2].forward()
    gather.arrive(1)
    for one in give:
        one.arrive(1)
    for one in (*give, gather, *x_ring, *h_ring):
        one.sent()
    for _, theirs in weights:
        theirs.wait_send()


def permutation():
    index = np.arange(ROWS).reshape(SIDE, SIDE, CAP).transpose(1, 0, 2).reshape(-1)
    return np.eye(ROWS, dtype=np.float32)[index]


def pair_permutations():
    out = np.zeros((2, SIDE * PAIR, BLOCK), np.float32)
    for c in range(2):
        for z in range(SIDE):
            out[c, z * PAIR + c * CAP + np.arange(CAP), z * CAP + np.arange(CAP)] = 1.0
    return out


def shards(tokens, expert_ids, route_weight, gate_weight, up_weight, down_weight, home_slot, spare_expert):
    ids = expert_ids.transpose(0, 2, 1)
    home_row = home_slot.reshape(1, SLOTS)
    piece_shape = jax.ShapeDtypeStruct((2, SIDE, SIDE, PIECE, 256), BF16)
    row_shape = jax.ShapeDtypeStruct((STEPS, 2, SIDE, SIDE, BLOCK, 256), BF16)
    one_shape = jax.ShapeDtypeStruct((2, SIDE, SIDE, BLOCK, 256), BF16)
    pair_shape = jax.ShapeDtypeStruct((2, 2, SIDE, SIDE, PAIR, 256), BF16)

    returned, returned_pair, landed, *_ = pl.pallas_call(
        main_kernel,
        out_shape=(one_shape, pair_shape, piece_shape, piece_shape),
        in_specs=[SM, SM, VM, VM, VM, VM, VM, HBM, HBM, HBM],
        out_specs=(HBM,) * 4,
        scratch_shapes=[
            pltpu.VMEM((2, 384, 4096), BF16),
            pltpu.VMEM((2, 384, 4096), BF16),
            pltpu.VMEM((2, 1536, 1024), BF16),
            pltpu.VMEM((4, ROWS, 4096), BF16),
            pltpu.VMEM((4, ROWS, 1536), BF16),
            pltpu.VMEM((STEPS, 2, ROWS, 512), BF16),
            pltpu.VMEM((STEPS, 4, ROWS, 512), BF16),
            pltpu.VMEM(row_shape.shape, BF16),
            pltpu.VMEM(row_shape.shape, BF16),
            pltpu.VMEM(row_shape.shape, BF16),
            pltpu.VMEM(one_shape.shape, BF16),
            pltpu.VMEM(pair_shape.shape, BF16),
            pltpu.VMEM(pair_shape.shape, BF16),
            pltpu.VMEM(piece_shape.shape, BF16),
            pltpu.VMEM(piece_shape.shape, BF16),
            pltpu.VMEM((2, ROWS, 384), F32),
            pltpu.SemaphoreType.DMA((7, 2, 2, 4)),
            pltpu.SemaphoreType.DMA((7, 2, 2, 4)),
            pltpu.SemaphoreType.DMA((4, 4)),
            pltpu.SemaphoreType.DMA((4, 4)),
            pltpu.SemaphoreType.DMA((4, 4)),
            pltpu.SemaphoreType.DMA((4, 4)),
            pltpu.SemaphoreType.DMA((6,)),
            pltpu.SemaphoreType.DMA((6,)),
            pltpu.SemaphoreType.DMA((3,)),
            pltpu.SemaphoreType.DMA((3,)),
            pltpu.SemaphoreType.DMA((3,)),
            pltpu.SemaphoreType.DMA((3, 3)),
            pltpu.SemaphoreType.REGULAR,
        ],
        compiler_params=pltpu.CompilerParams(
            collective_id=0, has_side_effects=True, vmem_limit_bytes=60 * 2**20
        ),
        name="exchange",
    )(
        home_slot,
        spare_expert,
        home_row,
        ids,
        tokens,
        jnp.asarray(permutation(), BF16),
        jnp.asarray(pair_permutations(), BF16),
        gate_weight,
        up_weight,
        down_weight,
    )

    return pl.pallas_call(
        mix_kernel,
        out_shape=(
            jax.ShapeDtypeStruct(tokens.shape, BF16),
            jax.ShapeDtypeStruct((1,) + gate_weight.shape[1:], BF16),
            jax.ShapeDtypeStruct((1,) + up_weight.shape[1:], BF16),
            jax.ShapeDtypeStruct((1,) + down_weight.shape[1:], BF16),
        ),
        in_specs=[VM, VM, VM, HBM, HBM, HBM],
        out_specs=(VM, HBM, HBM, HBM),
        scratch_shapes=[
            pltpu.VMEM(one_shape.shape, BF16),
            pltpu.VMEM(pair_shape.shape, BF16),
            pltpu.VMEM(piece_shape.shape, BF16),
            pltpu.VMEM(gate_weight.shape[1:], BF16),
            pltpu.VMEM(up_weight.shape[1:], BF16),
            pltpu.VMEM(down_weight.shape[1:], BF16),
            pltpu.SemaphoreType.DMA((4,)),
            pltpu.SemaphoreType.DMA((2, 3)),
        ],
        compiler_params=pltpu.CompilerParams(vmem_limit_bytes=60 * 2**20),
        name="mix",
    )(ids, route_weight.transpose(0, 2, 1), home_row, returned, returned_pair, landed)


def solution(mesh):
    placed = (
        P(None, "ep", "tp"),
        P(None, "ep", None),
        P(None, "ep", None),
        P("ep", "tp", None),
        P("ep", "tp", None),
        P("ep", None, "tp"),
        P(),
        P(),
    )
    return jax.shard_map(
        shards,
        mesh=mesh,
        in_specs=placed,
        out_specs=(
            P(None, "ep", "tp"),
            P("ep", "tp", None),
            P("ep", "tp", None),
            P("ep", None, "tp"),
        ),
        check_vma=False,
    )
```

```python
import functools

import jax
import jax.numpy as jnp
import numpy as np
from jax import lax
from jax.experimental import pallas as pl
from jax.experimental.pallas import tpu as pltpu
from jax.sharding import PartitionSpec as P

MESH = pl.DeviceIdType.MESH
BF16 = jnp.bfloat16
F32 = jnp.float32
STEPS = 2
SIDE = 4
CAP = 20
SLOTS = 64
TOK = 128
BLOCK = 4 * CAP
ROWS = 16 * CAP
PAIR = 48
PIECE = 288
HBM = pl.BlockSpec(memory_space=pltpu.MemorySpace.HBM)
VM = pl.BlockSpec(memory_space=pltpu.VMEM)
SM = pl.BlockSpec(memory_space=pltpu.SMEM)


def dot(a, b):
    return jnp.dot(a, b, preferred_element_type=F32)


def dot_t(a, b):
    return lax.dot_general(a, b, (((1,), (1,)), ((), ())), preferred_element_type=F32)


def dot_0(a, b):
    return lax.dot_general(a, b, (((0,), (0,)), ((), ())), preferred_element_type=F32)


def iota(shape, dim):
    return lax.broadcasted_iota(jnp.int32, shape, dim)


def slot_places(ids, home):
    to_slot = (home == iota((SLOTS, SLOTS), 0)).astype(BF16)
    before = (iota((TOK, TOK), 0) < iota((TOK, TOK), 1)).astype(BF16)
    named = iota((SLOTS, TOK), 0)
    picked = jnp.zeros((SLOTS, TOK), F32)
    for k in range(8):
        picked = jnp.where(ids[k : k + 1, :] == named, 1.0, picked)
    by_slot = dot(to_slot, picked.astype(BF16))
    position = dot(by_slot.astype(BF16), before)
    return jnp.where(by_slot > 0.5, position, -1.0).astype(BF16), to_slot


def rows_of(x):
    row = iota((ROWS, SLOTS), 0) + x * ROWS
    low = iota((ROWS, SLOTS), 1) * CAP
    spread = jnp.where((row >= low) & (row < low + CAP), 1.0, 0.0).astype(BF16)
    row = iota((ROWS, TOK), 0) + x * ROWS
    return spread, (row - ((row * 3277) >> 16) * CAP).astype(F32)


def pair_rows_of(x, i):
    def split(width):
        row = iota((SIDE * PAIR, width), 0)
        z = (row * 1366) >> 16
        rest = row - z * PAIR
        c = (rest * 3277) >> 16
        return z, rest, c

    z, rest, c = split(SLOTS)
    slot = (x * SIDE + z) * 4 + 2 * c + i
    spread = jnp.where((slot == iota((SIDE * PAIR, SLOTS), 1)) & (rest < 2 * CAP), 1.0, 0.0).astype(BF16)
    z, rest, c = split(TOK)
    return spread, jnp.where(rest < 2 * CAP, rest - c * CAP, -5).astype(F32)


def mix_kernel(
    ids_ref, rw_ref, home_ref, back_hbm, pair_hbm, pieces, mixed_ref, gate, up, down,
    back, back_pair, held, gate_v, up_v, down_v, in_sem, out_sem,
):
    loads = [
        pltpu.make_async_copy(back_hbm, back, in_sem.at[0]),
        pltpu.make_async_copy(pair_hbm, back_pair, in_sem.at[1]),
    ]
    loads += [pltpu.make_async_copy(pieces.at[h], held.at[h], in_sem.at[2 + h]) for h in range(2)]
    for c in loads:
        c.start()
    writes = []

    def join(h):
        loads[2 + h].wait()

        def one(p, _):
            of = held.at[h, p // SIDE, lax.rem(p, SIDE)]
            columns = pl.ds(pl.multiple_of(p * 256, 256), 256)
            low = pl.ds(pl.multiple_of(h * 768 + p * 48, 16), 48)
            gate_v[pl.ds(h * 96, 96), columns] = of[pl.ds(0, 96)]
            up_v[pl.ds(h * 96, 96), columns] = of[pl.ds(96, 96)]
            down_v[low, pl.ds(0, 256)] = of[pl.ds(192, 48)]
            down_v[low, pl.ds(256, 256)] = of[pl.ds(240, 48)]
            return 0

        lax.fori_loop(0, 16, one, 0)
        for n, (a, b, rows) in enumerate(((gate_v, gate, 96), (up_v, up, 96), (down_v, down, 768))):
            part = pl.ds(h * rows, rows)
            writes.append(pltpu.make_async_copy(a.at[part], b.at[0, part], out_sem.at[h, n]))
            writes[-1].start()

    def mix(s):
        places, to_slot = slot_places(ids_ref[s], home_ref[...])
        named = iota((SLOTS, TOK), 0)
        scale = jnp.zeros((SLOTS, TOK), F32)
        for k in range(8):
            scale = jnp.where(ids_ref[s, k : k + 1, :] == named, rw_ref[s, k : k + 1, :], scale)
        high = scale.astype(BF16)
        rest = (scale - high.astype(F32)).astype(BF16)
        high = dot(to_slot, high).astype(BF16)
        rest = dot(to_slot, rest).astype(BF16)
        totals = [jnp.zeros((TOK, 256), F32)] * 2
        loads[s].wait()
        parts = [(x, i) for x in range(SIDE) for i in range(2 if s else 1)]
        for x, i in parts:
            spread, within = pair_rows_of(x, i) if s else rows_of(x)
            here = dot(spread, places) == within
            high_row = jnp.where(here, dot(spread, high), 0.0).astype(BF16)
            rest_row = jnp.where(here, dot(spread, rest), 0.0).astype(BF16)
            for h in range(2):
                block = back_pair[i, h, x].reshape(SIDE * PAIR, 256) if s else back[h, x].reshape(ROWS, 256)
                totals[h] = totals[h] + dot_0(high_row, block) + dot_0(rest_row, block)
        for h in range(2):
            mixed_ref[s, :, h * 256 : (h + 1) * 256] = totals[h].astype(BF16)

    mix(0)
    join(0)
    join(1)
    mix(1)
    for c in writes:
        c.wait()


class Exchange:
    def __init__(self, number, src, mid, dst, send, recv):
        ep, tp = lax.axis_index("ep"), lax.axis_index("tp")
        self.ex, self.ez, self.tp = ep // SIDE, lax.rem(ep, SIDE), tp
        self.src, self.mid, self.dst = src, mid, dst
        self.send, self.recv, self.number = send, recv, number
        self.started = []

    def copy(self, phase, half, d):
        ex, ez = self.ex, self.ez
        along_x = half == phase
        x = lax.rem(ex + d, SIDE) if along_x else ex
        z = ez if along_x else lax.rem(ez + d, SIDE)
        if phase == 0:
            a = self.src.at[0, x] if half == 0 else self.src.at[1, :, z]
            b = self.mid.at[half, ex if half == 0 else ez]
        else:
            a = self.mid.at[half, :, z if half == 0 else x]
            b = self.dst.at[0, :, ez] if half == 0 else self.dst.at[1, ex]
        send = self.send.at[self.number, phase, half, d]
        if d == 0:
            return pltpu.make_async_copy(a, b, send)
        recv = self.recv.at[self.number, phase, half, d]
        return pltpu.make_async_remote_copy(
            a, b, send, recv, device_id=(x * SIDE + z, self.tp), device_id_type=MESH
        )

    def start(self, phase):
        for d in (2, 1, 3, 0):
            for half in range(2):
                c = self.copy(phase, half, d)
                c.start()
                self.started.append((phase, d, c))

    def arrive(self, phase):
        for at, d, c in self.started:
            if at == phase:
                c.wait() if d == 0 else c.wait_recv()

    def forward(self):
        self.arrive(0)
        self.start(1)

    def sent(self):
        for _, d, c in self.started:
            if d:
                c.wait_send()


class Ring:
    def __init__(self, number, ref, width, send, recv):
        self.ep, self.tp = lax.axis_index("ep"), lax.axis_index("tp")
        self.y = self.tp // 2
        self.ref, self.width, self.number = ref, width, number
        self.send, self.recv = send, recv
        self.all = {}

    def copy(self, kind):
        y = lax.rem(self.y + (0, 0, 3, 1)[kind], 4)
        to = lax.rem(self.tp + (2, 6, 2, 6)[kind], 8)
        rows = (pl.ds(0, ROWS), pl.ds(0, ROWS), pl.ds(0, ROWS // 2), pl.ds(ROWS // 2, ROWS // 2))[kind]
        part = self.ref.at[rows, pl.ds(pl.multiple_of(y * self.width, 128), self.width)]
        return pltpu.make_async_remote_copy(
            part,
            part,
            self.send.at[self.number, kind],
            self.recv.at[self.number, kind],
            device_id=(self.ep, to),
            device_id_type=MESH,
        )

    def start(self):
        for kind in (0, 1):
            self.all[kind] = self.copy(kind)
            self.all[kind].start()

    def forward(self):
        for kind in (0, 1):
            self.all[kind].wait_recv()
            self.all[kind + 2] = self.copy(kind + 2)
            self.all[kind + 2].start()

    def arrive(self):
        for kind in (2, 3):
            self.all[kind].wait_recv()

    def sent(self):
        for c in self.all.values():
            c.wait_send()


def main_kernel(
    home_s, spare_s, home_ref, ids_ref, tok_ref, perm, pair_perm, wg, wu, wd,
    returned, returned_pair, landed, mid_a,
    gate_w, up_w, down_w, xs, hs, swap, outs, arrived, outgoing, mid_d, mid_r, out_pair, mid_pair, spread, chosen, acc,
    a_send, a_recv, x_send, x_recv, h_send, h_recv, c_send, c_recv, w_send, w_recv, w_local, p_local, credit,
):
    ep, tp = lax.axis_index("ep"), lax.axis_index("tp")
    ex, ez = ep // SIDE, lax.rem(ep, SIDE)
    core = lax.rem(tp, 2)
    mate = (ep, tp + 1 - 2 * core)

    barrier = pltpu.get_barrier_semaphore()
    for d in range(1, SIDE):
        pl.semaphore_signal(barrier, inc=1, device_id=(lax.rem(ex + d, SIDE) * SIDE + ez, tp), device_id_type=MESH)
        pl.semaphore_signal(barrier, inc=1, device_id=(ex * SIDE + lax.rem(ez + d, SIDE), tp), device_id_type=MESH)
    pl.semaphore_signal(barrier, inc=1, device_id=(ep, lax.rem(tp + 2, 8)), device_id_type=MESH)
    pl.semaphore_signal(barrier, inc=1, device_id=(ep, lax.rem(tp + 6, 8)), device_id_type=MESH)
    pl.semaphore_signal(barrier, inc=1, device_id=mate, device_id_type=MESH)

    deal = [Exchange(s, outgoing.at[s], mid_d.at[s], arrived.at[s], a_send, a_recv) for s in range(STEPS)]
    give = [Exchange(2, outgoing.at[0], mid_r, returned, a_send, a_recv)]
    for i in range(2):
        give.append(Exchange(3 + i, out_pair.at[i], mid_pair.at[i], returned_pair.at[i], a_send, a_recv))
    scatter = Exchange(5, chosen, mid_a, spread, a_send, a_recv)
    gather = Exchange(6, chosen, spread, landed, a_send, a_recv)
    x_ring = [Ring(q, xs.at[q], 1024, x_send, x_recv) for q in range(4)]
    h_ring = [Ring(q, hs.at[q], 384, h_send, h_recv) for q in range(4)]

    own_two, mate_two = pl.ds(2 * core, 2), pl.ds(2 - 2 * core, 2)
    own_rows = pl.ds(pl.multiple_of(core * 192, 16), 192)
    own_half = pl.ds(pl.multiple_of(core * 512, 512), 512)
    mate_half = pl.ds(pl.multiple_of(512 - core * 512, 512), 512)
    weights = []
    for n, (w, held) in enumerate(((wg, gate_w), (wu, up_w), (wd, down_w))):
        to = held.at[:, :, own_half] if n == 2 else held.at[:, own_rows]
        mine = pltpu.make_async_copy(w.at[own_two], to, w_local.at[n])
        theirs = pltpu.make_async_remote_copy(
            w.at[mate_two], to, w_send.at[n], w_recv.at[n], device_id=mate, device_id_type=MESH
        )
        weights.append((mine, theirs))

    own_perm = pl.ds(pl.multiple_of(core * 160, 16), 160)
    mate_perm = pl.ds(pl.multiple_of(160 - core * 160, 16), 160)

    def regroup(s):
        def one(g, _):
            rows = pl.ds(pl.multiple_of(g * BLOCK, 16), BLOCK)
            for h in range(2):
                block = arrived[s, h, g].reshape(ROWS, 256)
                mine = dot(perm[own_perm, :], block).astype(BF16)
                theirs = dot(perm[mate_perm, :], block).astype(BF16)
                columns = pl.ds(pl.multiple_of(tp * 512 + h * 256, 256), 256)
                for i in range(2):
                    xs[2 * s + i, rows, columns] = mine[i * BLOCK : (i + 1) * BLOCK]
                    swap[s, i, rows, pl.ds(h * 256, 256)] = theirs[i * BLOCK : (i + 1) * BLOCK]
            return 0

        lax.fori_loop(0, SIDE, one, 0)
        c = pltpu.make_async_remote_copy(
            swap.at[s],
            xs.at[pl.ds(2 * s, 2), :, pl.ds(pl.multiple_of(tp * 512, 512), 512)],
            c_send.at[s],
            c_recv.at[s],
            device_id=mate,
            device_id_type=MESH,
        )
        c.start()
        return c

    def hidden(q):
        i = q % 2
        acc[...] = jnp.zeros_like(acc)

        def one(k, _):
            columns = pl.ds(pl.multiple_of(k * 512, 512), 512)
            block = xs[q, :, columns]
            acc[0] += dot_t(block, gate_w[i, :, columns])
            acc[1] += dot_t(block, up_w[i, :, columns])
            return 0

        lax.fori_loop(0, 8, one, 0)
        columns = pl.ds(pl.multiple_of((tp // 2) * 384, 128), 384)
        gate = acc[0]
        hs[q, :, columns] = (gate / (1.0 + jnp.exp(-gate)) * acc[1]).astype(BF16)
        h_ring[q].start()

    def out(q):
        s, i = q // 2, q % 2

        def one(n, _):
            columns = pl.ds(pl.multiple_of(n * 256, 256), 256)
            mine = pl.ds(pl.multiple_of(core * 512 + n * 256, 256), 256)
            theirs = pl.ds(pl.multiple_of(512 - core * 512 + n * 256, 256), 256)
            block = hs[q]
            swap[s, i, :, columns] = dot(block, down_w[i, :, theirs]).astype(BF16)
            outs[s, 2 * core + i, :, columns] = dot(block, down_w[i, :, mine]).astype(BF16)
            return 0

        lax.fori_loop(0, 2, one, 0)
        c = pltpu.make_async_remote_copy(
            swap.at[s, i],
            outs.at[s, 2 * core + i],
            c_send.at[2 + q],
            c_recv.at[2 + q],
            device_id=mate,
            device_id_type=MESH,
        )
        c.start()
        return c

    def ungroup():
        def one(g, _):
            rows = pl.ds(pl.multiple_of(g * BLOCK, 16), BLOCK)
            for h in range(2):
                block = outs[0, :, rows, pl.ds(h * 256, 256)].reshape(ROWS, 256)
                outgoing[0, h, g] = dot(perm[...], block).astype(BF16).reshape(SIDE, BLOCK, 256)
            return 0

        lax.fori_loop(0, SIDE, one, 0)
        give[0].start(0)

    def ungroup_pair(i):
        def one(g, _):
            rows = pl.ds(pl.multiple_of(g * BLOCK, 16), BLOCK)
            for h in range(2):
                columns = pl.ds(h * 256, 256)
                total = dot(pair_perm[0], outs[1, i, rows, columns]) + dot(pair_perm[1], outs[1, 2 + i, rows, columns])
                out_pair[i, h, g] = total.astype(BF16).reshape(SIDE, PAIR, 256)
            return 0

        lax.fori_loop(0, SIDE, one, 0)
        give[1 + i].start(0)

    def choose():
        def one(d, _):
            x, z = d // SIDE, lax.rem(d, SIDE)
            home = home_s[spare_s[d]] // 4
            for h in range(2):
                chosen[h, x, z] = spread[h, home // SIDE, lax.rem(home, SIDE)]
            return 0

        lax.fori_loop(0, 16, one, 0)
        for d in range(1, SIDE):
            along_x, along_z = lax.rem(ex + d, SIDE) * SIDE + ez, ex * SIDE + lax.rem(ez + d, SIDE)
            pl.semaphore_signal(credit, inc=1, device_id=(along_x, tp), device_id_type=MESH)
            pl.semaphore_signal(credit, inc=1, device_id=(along_z, tp), device_id_type=MESH)
        pl.semaphore_wait(credit, 6)
        gather.start(0)

    def place(s):
        places, _ = slot_places(ids_ref[s], home_ref[...])

        def one(x, _):
            spread_rows, within = rows_of(x)
            placing = jnp.where(dot(spread_rows, places) == within, 1.0, 0.0).astype(BF16)
            for h in range(2):
                block = dot(placing, tok_ref[s, :, h * 256 : (h + 1) * 256]).astype(BF16)
                outgoing[s, h, x] = block.reshape(SIDE, BLOCK, 256)
            return 0

        lax.fori_loop(0, SIDE, one, 0)

    def fetch(j):
        h, two, b = j // 8, lax.rem(j, 8), lax.rem(j, 3)
        rows = pl.ds(pl.multiple_of(h * 96, 16), 96)
        columns = pl.ds(pl.multiple_of(two * 512, 512), 512)
        low = pl.ds(pl.multiple_of(h * 768 + two * 96, 16), 96)
        to = pl.ds(pl.multiple_of(b * 96, 16), 96)
        return [
            pltpu.make_async_copy(wg.at[:, rows, columns], hs.at[:, to, pl.ds(0, 512)], p_local.at[b, 0]),
            pltpu.make_async_copy(wu.at[:, rows, columns], hs.at[:, to, pl.ds(512, 512)], p_local.at[b, 1]),
            pltpu.make_async_copy(wd.at[:, low, :], hs.at[:, to, pl.ds(1024, 512)], p_local.at[b, 2]),
        ]

    def fetch_start(j):
        for c in fetch(j):
            c.start()

    def cut(first, end):
        def find(d, own):
            slot = home_s[spare_s[d]]
            return jnp.maximum(own, jnp.where(slot // 4 == ep, lax.rem(slot, 4), 0))

        own = lax.fori_loop(0, 16, find, jnp.int32(0))

        def one(j, _):
            for c in fetch(j):
                c.wait()
            h, two, b = j // 8, lax.rem(j, 8), lax.rem(j, 3)
            px, pair = two // 2, lax.rem(two, 2)

            def pick(low, rows, columns):
                at = pl.ds(pl.multiple_of(b * 96 + low, 16), rows)
                value = hs[0, at, columns]
                for k in range(1, 4):
                    value = jnp.where(own == k, hs[k, at, columns], value)
                return value

            for z in range(2):
                to = chosen.at[h, px, 2 * pair + z]
                for n in range(2):
                    to[pl.ds(96 * n, 96)] = pick(0, 96, pl.ds(512 * n + 256 * z, 256))
                    to[pl.ds(192 + 48 * n, 48)] = pick(48 * z, 48, pl.ds(1024 + 256 * n, 256))
            return 0

        def more(j, _):
            one(j, 0)
            fetch_start(j + 3)
            return 0

        lax.fori_loop(first, min(end, 13), more, 0)
        if end == 16:
            lax.fori_loop(13, 16, one, 0)

    for j in range(3):
        fetch_start(j)
    place(0)
    pl.semaphore_wait(barrier, 9)
    deal[0].start(0)
    for mine, theirs in weights:
        theirs.start()
        mine.start()
    deal[0].forward()
    place(1)
    deal[0].arrive(1)
    swap_x = [regroup(0)]
    deal[1].start(0)
    swap_x[0].wait()
    x_ring[0].start()
    cut(0, 8)
    deal[1].forward()
    cut(8, 16)
    scatter.start(0)
    x_ring[0].forward()
    x_ring[1].start()
    for mine, theirs in weights:
        mine.wait()
        theirs.wait_recv()
    x_ring[0].arrive()
    hidden(0)
    deal[1].arrive(1)
    swap_x.append(regroup(1))
    swap_x[1].wait()
    x_ring[1].forward()
    x_ring[2].start()
    h_ring[0].forward()
    scatter.forward()
    x_ring[1].arrive()
    hidden(1)
    h_ring[0].arrive()
    swap_o = [out(0)]
    x_ring[2].forward()
    x_ring[3].start()
    h_ring[1].forward()
    scatter.arrive(1)
    scatter.sent()
    choose()
    x_ring[2].arrive()
    hidden(2)
    h_ring[1].arrive()
    swap_o.append(out(1))
    swap_o[0].wait()
    swap_o[1].wait()
    for one in deal:
        one.sent()
    ungroup()
    x_ring[3].forward()
    h_ring[2].forward()
    gather.forward()
    x_ring[3].arrive()
    hidden(3)
    give[0].forward()
    h_ring[2].arrive()
    swap_o.append(out(2))
    swap_o[2].wait()
    ungroup_pair(0)
    h_ring[3].forward()
    h_ring[3].arrive()
    swap_o.append(out(3))
    swap_o[3].wait()
    ungroup_pair(1)
    give[1].forward()
    give[2].forward()
    gather.arrive(1)
    for one in give:
        one.arrive(1)
    for one in (*give, gather, *x_ring, *h_ring):
        one.sent()
    for _, theirs in weights:
        theirs.wait_send()


def permutation():
    index = np.arange(ROWS).reshape(SIDE, SIDE, CAP).transpose(1, 0, 2).reshape(-1)
    return np.eye(ROWS, dtype=np.float32)[index]


def pair_permutations():
    out = np.zeros((2, SIDE * PAIR, BLOCK), np.float32)
    for c in range(2):
        for z in range(SIDE):
            out[c, z * PAIR + c * CAP + np.arange(CAP), z * CAP + np.arange(CAP)] = 1.0
    return out


def shards(tokens, expert_ids, route_weight, gate_weight, up_weight, down_weight, home_slot, spare_expert):
    ids = expert_ids.transpose(0, 2, 1)
    home_row = home_slot.reshape(1, SLOTS)
    piece_shape = jax.ShapeDtypeStruct((2, SIDE, SIDE, PIECE, 256), BF16)
    row_shape = jax.ShapeDtypeStruct((STEPS, 2, SIDE, SIDE, BLOCK, 256), BF16)
    one_shape = jax.ShapeDtypeStruct((2, SIDE, SIDE, BLOCK, 256), BF16)
    pair_shape = jax.ShapeDtypeStruct((2, 2, SIDE, SIDE, PAIR, 256), BF16)

    returned, returned_pair, landed, *_ = pl.pallas_call(
        main_kernel,
        out_shape=(one_shape, pair_shape, piece_shape, piece_shape),
        in_specs=[SM, SM, VM, VM, VM, VM, VM, HBM, HBM, HBM],
        out_specs=(HBM,) * 4,
        scratch_shapes=[
            pltpu.VMEM((2, 384, 4096), BF16),
            pltpu.VMEM((2, 384, 4096), BF16),
            pltpu.VMEM((2, 1536, 1024), BF16),
            pltpu.VMEM((4, ROWS, 4096), BF16),
            pltpu.VMEM((4, ROWS, 1536), BF16),
            pltpu.VMEM((STEPS, 2, ROWS, 512), BF16),
            pltpu.VMEM((STEPS, 4, ROWS, 512), BF16),
            pltpu.VMEM(row_shape.shape, BF16),
            pltpu.VMEM(row_shape.shape, BF16),
            pltpu.VMEM(row_shape.shape, BF16),
            pltpu.VMEM(one_shape.shape, BF16),
            pltpu.VMEM(pair_shape.shape, BF16),
            pltpu.VMEM(pair_shape.shape, BF16),
            pltpu.VMEM(piece_shape.shape, BF16),
            pltpu.VMEM(piece_shape.shape, BF16),
            pltpu.VMEM((2, ROWS, 384), F32),
            pltpu.SemaphoreType.DMA((7, 2, 2, 4)),
            pltpu.SemaphoreType.DMA((7, 2, 2, 4)),
            pltpu.SemaphoreType.DMA((4, 4)),
            pltpu.SemaphoreType.DMA((4, 4)),
            pltpu.SemaphoreType.DMA((4, 4)),
            pltpu.SemaphoreType.DMA((4, 4)),
            pltpu.SemaphoreType.DMA((6,)),
            pltpu.SemaphoreType.DMA((6,)),
            pltpu.SemaphoreType.DMA((3,)),
            pltpu.SemaphoreType.DMA((3,)),
            pltpu.SemaphoreType.DMA((3,)),
            pltpu.SemaphoreType.DMA((3, 3)),
            pltpu.SemaphoreType.REGULAR,
        ],
        compiler_params=pltpu.CompilerParams(
            collective_id=0, has_side_effects=True, vmem_limit_bytes=60 * 2**20
        ),
        name="exchange",
    )(
        home_slot,
        spare_expert,
        home_row,
        ids,
        tokens,
        jnp.asarray(permutation(), BF16),
        jnp.asarray(pair_permutations(), BF16),
        gate_weight,
        up_weight,
        down_weight,
    )

    return pl.pallas_call(
        mix_kernel,
        out_shape=(
            jax.ShapeDtypeStruct(tokens.shape, BF16),
            jax.ShapeDtypeStruct((1,) + gate_weight.shape[1:], BF16),
            jax.ShapeDtypeStruct((1,) + up_weight.shape[1:], BF16),
            jax.ShapeDtypeStruct((1,) + down_weight.shape[1:], BF16),
        ),
        in_specs=[VM, VM, VM, HBM, HBM, HBM],
        out_specs=(VM, HBM, HBM, HBM),
        scratch_shapes=[
            pltpu.VMEM(one_shape.shape, BF16),
            pltpu.VMEM(pair_shape.shape, BF16),
            pltpu.VMEM(piece_shape.shape, BF16),
            pltpu.VMEM(gate_weight.shape[1:], BF16),
            pltpu.VMEM(up_weight.shape[1:], BF16),
            pltpu.VMEM(down_weight.shape[1:], BF16),
            pltpu.SemaphoreType.DMA((4,)),
            pltpu.SemaphoreType.DMA((2, 3)),
        ],
        compiler_params=pltpu.CompilerParams(vmem_limit_bytes=60 * 2**20),
        name="mix",
    )(ids, route_weight.transpose(0, 2, 1), home_row, returned, returned_pair, landed)


def solution(mesh):
    placed = (
        P(None, "ep", "tp"),
        P(None, "ep", None),
        P(None, "ep", None),
        P("ep", "tp", None),
        P("ep", "tp", None),
        P("ep", None, "tp"),
        P(),
        P(),
    )
    return jax.shard_map(
        shards,
        mesh=mesh,
        in_specs=placed,
        out_specs=(
            P(None, "ep", "tp"),
            P("ep", "tp", None),
            P("ep", "tp", None),
            P("ep", None, "tp"),
        ),
        check_vma=False,
    )
```

```python
import functools

import jax
import jax.numpy as jnp
import numpy as np
from jax import lax
from jax.experimental import pallas as pl
from jax.experimental.pallas import tpu as pltpu
from jax.sharding import PartitionSpec as P

MESH = pl.DeviceIdType.MESH
BF16 = jnp.bfloat16
F32 = jnp.float32
STEPS = 2
SIDE = 4
CAP = 20
SLOTS = 64
TOK = 128
BLOCK = 4 * CAP
ROWS = 16 * CAP
PAIR = 48
PIECE = 288
HBM = pl.BlockSpec(memory_space=pltpu.MemorySpace.HBM)
VM = pl.BlockSpec(memory_space=pltpu.VMEM)
SM = pl.BlockSpec(memory_space=pltpu.SMEM)


def dot(a, b):
    return jnp.dot(a, b, preferred_element_type=F32)


def dot_t(a, b):
    return lax.dot_general(a, b, (((1,), (1,)), ((), ())), preferred_element_type=F32)


def dot_0(a, b):
    return lax.dot_general(a, b, (((0,), (0,)), ((), ())), preferred_element_type=F32)


def iota(shape, dim):
    return lax.broadcasted_iota(jnp.int32, shape, dim)


def slot_places(ids, home):
    to_slot = (home == iota((SLOTS, SLOTS), 0)).astype(BF16)
    before = (iota((TOK, TOK), 0) < iota((TOK, TOK), 1)).astype(BF16)
    named = iota((SLOTS, TOK), 0)
    picked = jnp.zeros((SLOTS, TOK), F32)
    for k in range(8):
        picked = jnp.where(ids[k : k + 1, :] == named, 1.0, picked)
    by_slot = dot(to_slot, picked.astype(BF16))
    position = dot(by_slot.astype(BF16), before)
    return jnp.where(by_slot > 0.5, position, -1.0).astype(BF16), to_slot


def rows_of(x):
    row = iota((ROWS, SLOTS), 0) + x * ROWS
    low = iota((ROWS, SLOTS), 1) * CAP
    spread = jnp.where((row >= low) & (row < low + CAP), 1.0, 0.0).astype(BF16)
    row = iota((ROWS, TOK), 0) + x * ROWS
    return spread, (row - ((row * 3277) >> 16) * CAP).astype(F32)


def pair_rows_of(x, i):
    def split(width):
        row = iota((SIDE * PAIR, width), 0)
        z = (row * 1366) >> 16
        rest = row - z * PAIR
        c = (rest * 3277) >> 16
        return z, rest, c

    z, rest, c = split(SLOTS)
    slot = (x * SIDE + z) * 4 + 2 * c + i
    spread = jnp.where((slot == iota((SIDE * PAIR, SLOTS), 1)) & (rest < 2 * CAP), 1.0, 0.0).astype(BF16)
    z, rest, c = split(TOK)
    return spread, jnp.where(rest < 2 * CAP, rest - c * CAP, -5).astype(F32)


def mix_kernel(
    ids_ref, rw_ref, home_ref, back_hbm, pair_hbm, pieces, mixed_ref, gate, up, down,
    back, back_pair, held, gate_v, up_v, down_v, in_sem, out_sem,
):
    loads = [
        pltpu.make_async_copy(back_hbm, back, in_sem.at[0]),
        pltpu.make_async_copy(pair_hbm, back_pair, in_sem.at[1]),
    ]
    loads += [pltpu.make_async_copy(pieces.at[h], held.at[h], in_sem.at[2 + h]) for h in range(2)]
    for c in loads:
        c.start()
    writes = []

    def join(h):
        loads[2 + h].wait()

        def one(p, _):
            of = held.at[h, p // SIDE, lax.rem(p, SIDE)]
            columns = pl.ds(pl.multiple_of(p * 256, 256), 256)
            low = pl.ds(pl.multiple_of(h * 768 + p * 48, 16), 48)
            gate_v[pl.ds(h * 96, 96), columns] = of[pl.ds(0, 96)]
            up_v[pl.ds(h * 96, 96), columns] = of[pl.ds(96, 96)]
            down_v[low, pl.ds(0, 256)] = of[pl.ds(192, 48)]
            down_v[low, pl.ds(256, 256)] = of[pl.ds(240, 48)]
            return 0

        lax.fori_loop(0, 16, one, 0)
        for n, (a, b, rows) in enumerate(((gate_v, gate, 96), (up_v, up, 96), (down_v, down, 768))):
            part = pl.ds(h * rows, rows)
            writes.append(pltpu.make_async_copy(a.at[part], b.at[0, part], out_sem.at[h, n]))
            writes[-1].start()

    def mix(s):
        places, to_slot = slot_places(ids_ref[s], home_ref[...])
        named = iota((SLOTS, TOK), 0)
        scale = jnp.zeros((SLOTS, TOK), F32)
        for k in range(8):
            scale = jnp.where(ids_ref[s, k : k + 1, :] == named, rw_ref[s, k : k + 1, :], scale)
        high = scale.astype(BF16)
        rest = (scale - high.astype(F32)).astype(BF16)
        high = dot(to_slot, high).astype(BF16)
        rest = dot(to_slot, rest).astype(BF16)
        totals = [jnp.zeros((TOK, 256), F32)] * 2
        loads[s].wait()
        parts = [(x, i) for x in range(SIDE) for i in range(2 if s else 1)]
        for x, i in parts:
            spread, within = pair_rows_of(x, i) if s else rows_of(x)
            here = dot(spread, places) == within
            high_row = jnp.where(here, dot(spread, high), 0.0).astype(BF16)
            rest_row = jnp.where(here, dot(spread, rest), 0.0).astype(BF16)
            for h in range(2):
                block = back_pair[i, h, x].reshape(SIDE * PAIR, 256) if s else back[h, x].reshape(ROWS, 256)
                totals[h] = totals[h] + dot_0(high_row, block) + dot_0(rest_row, block)
        for h in range(2):
            mixed_ref[s, :, h * 256 : (h + 1) * 256] = totals[h].astype(BF16)

    mix(0)
    join(0)
    join(1)
    mix(1)
    for c in writes:
        c.wait()


class Exchange:
    def __init__(self, number, src, mid, dst, send, recv):
        ep, tp = lax.axis_index("ep"), lax.axis_index("tp")
        self.ex, self.ez, self.tp = ep // SIDE, lax.rem(ep, SIDE), tp
        self.src, self.mid, self.dst = src, mid, dst
        self.send, self.recv, self.number = send, recv, number
        self.started = []

    def copy(self, phase, half, d):
        ex, ez = self.ex, self.ez
        along_x = half == phase
        x = lax.rem(ex + d, SIDE) if along_x else ex
        z = ez if along_x else lax.rem(ez + d, SIDE)
        if phase == 0:
            a = self.src.at[0, x] if half == 0 else self.src.at[1, :, z]
            b = self.mid.at[half, ex if half == 0 else ez]
        else:
            a = self.mid.at[half, :, z if half == 0 else x]
            b = self.dst.at[0, :, ez] if half == 0 else self.dst.at[1, ex]
        send = self.send.at[self.number, phase, half, d]
        if d == 0:
            return pltpu.make_async_copy(a, b, send)
        recv = self.recv.at[self.number, phase, half, d]
        return pltpu.make_async_remote_copy(
            a, b, send, recv, device_id=(x * SIDE + z, self.tp), device_id_type=MESH
        )

    def start(self, phase):
        for d in (1, 3, 2, 0):
            for half in range(2):
                c = self.copy(phase, half, d)
                c.start()
                self.started.append((phase, d, c))

    def arrive(self, phase):
        for at, d, c in self.started:
            if at == phase:
                c.wait() if d == 0 else c.wait_recv()

    def forward(self):
        self.arrive(0)
        self.start(1)

    def sent(self):
        for _, d, c in self.started:
            if d:
                c.wait_send()


class Ring:
    def __init__(self, number, ref, width, send, recv):
        self.ep, self.tp = lax.axis_index("ep"), lax.axis_index("tp")
        self.y = self.tp // 2
        self.ref, self.width, self.number = ref, width, number
        self.send, self.recv = send, recv
        self.all = {}

    def copy(self, kind):
        y = lax.rem(self.y + (0, 0, 3, 1)[kind], 4)
        to = lax.rem(self.tp + (2, 6, 2, 6)[kind], 8)
        rows = (pl.ds(0, ROWS), pl.ds(0, ROWS), pl.ds(0, ROWS // 2), pl.ds(ROWS // 2, ROWS // 2))[kind]
        part = self.ref.at[rows, pl.ds(pl.multiple_of(y * self.width, 128), self.width)]
        return pltpu.make_async_remote_copy(
            part,
            part,
            self.send.at[self.number, kind],
            self.recv.at[self.number, kind],
            device_id=(self.ep, to),
            device_id_type=MESH,
        )

    def start(self):
        for kind in (0, 1):
            self.all[kind] = self.copy(kind)
            self.all[kind].start()

    def forward(self):
        for kind in (0, 1):
            self.all[kind].wait_recv()
            self.all[kind + 2] = self.copy(kind + 2)
            self.all[kind + 2].start()

    def arrive(self):
        for kind in (2, 3):
            self.all[kind].wait_recv()

    def sent(self):
        for c in self.all.values():
            c.wait_send()


def main_kernel(
    home_s, spare_s, home_ref, ids_ref, tok_ref, perm, pair_perm, wg, wu, wd,
    returned, returned_pair, landed, mid_a,
    gate_w, up_w, down_w, xs, hs, swap, outs, arrived, outgoing, mid_d, mid_r, out_pair, mid_pair, spread, chosen, acc,
    a_send, a_recv, x_send, x_recv, h_send, h_recv, c_send, c_recv, w_send, w_recv, w_local, p_local, credit,
):
    ep, tp = lax.axis_index("ep"), lax.axis_index("tp")
    ex, ez = ep // SIDE, lax.rem(ep, SIDE)
    core = lax.rem(tp, 2)
    mate = (ep, tp + 1 - 2 * core)

    barrier = pltpu.get_barrier_semaphore()
    for d in range(1, SIDE):
        pl.semaphore_signal(barrier, inc=1, device_id=(lax.rem(ex + d, SIDE) * SIDE + ez, tp), device_id_type=MESH)
        pl.semaphore_signal(barrier, inc=1, device_id=(ex * SIDE + lax.rem(ez + d, SIDE), tp), device_id_type=MESH)
    pl.semaphore_signal(barrier, inc=1, device_id=(ep, lax.rem(tp + 2, 8)), device_id_type=MESH)
    pl.semaphore_signal(barrier, inc=1, device_id=(ep, lax.rem(tp + 6, 8)), device_id_type=MESH)
    pl.semaphore_signal(barrier, inc=1, device_id=mate, device_id_type=MESH)

    deal = [Exchange(s, outgoing.at[s], mid_d.at[s], arrived.at[s], a_send, a_recv) for s in range(STEPS)]
    give = [Exchange(2, outgoing.at[0], mid_r, returned, a_send, a_recv)]
    for i in range(2):
        give.append(Exchange(3 + i, out_pair.at[i], mid_pair.at[i], returned_pair.at[i], a_send, a_recv))
    scatter = Exchange(5, chosen, mid_a, spread, a_send, a_recv)
    gather = Exchange(6, chosen, spread, landed, a_send, a_recv)
    x_ring = [Ring(q, xs.at[q], 1024, x_send, x_recv) for q in range(4)]
    h_ring = [Ring(q, hs.at[q], 384, h_send, h_recv) for q in range(4)]

    own_two, mate_two = pl.ds(2 * core, 2), pl.ds(2 - 2 * core, 2)
    own_rows = pl.ds(pl.multiple_of(core * 192, 16), 192)
    own_half = pl.ds(pl.multiple_of(core * 512, 512), 512)
    mate_half = pl.ds(pl.multiple_of(512 - core * 512, 512), 512)
    weights = []
    for n, (w, held) in enumerate(((wg, gate_w), (wu, up_w), (wd, down_w))):
        to = held.at[:, :, own_half] if n == 2 else held.at[:, own_rows]
        mine = pltpu.make_async_copy(w.at[own_two], to, w_local.at[n])
        theirs = pltpu.make_async_remote_copy(
            w.at[mate_two], to, w_send.at[n], w_recv.at[n], device_id=mate, device_id_type=MESH
        )
        weights.append((mine, theirs))

    own_perm = pl.ds(pl.multiple_of(core * 160, 16), 160)
    mate_perm = pl.ds(pl.multiple_of(160 - core * 160, 16), 160)

    def regroup(s):
        def one(g, _):
            rows = pl.ds(pl.multiple_of(g * BLOCK, 16), BLOCK)
            for h in range(2):
                block = arrived[s, h, g].reshape(ROWS, 256)
                mine = dot(perm[own_perm, :], block).astype(BF16)
                theirs = dot(perm[mate_perm, :], block).astype(BF16)
                columns = pl.ds(pl.multiple_of(tp * 512 + h * 256, 256), 256)
                for i in range(2):
                    xs[2 * s + i, rows, columns] = mine[i * BLOCK : (i + 1) * BLOCK]
                    swap[s, i, rows, pl.ds(h * 256, 256)] = theirs[i * BLOCK : (i + 1) * BLOCK]
            return 0

        lax.fori_loop(0, SIDE, one, 0)
        c = pltpu.make_async_remote_copy(
            swap.at[s],
            xs.at[pl.ds(2 * s, 2), :, pl.ds(pl.multiple_of(tp * 512, 512), 512)],
            c_send.at[s],
            c_recv.at[s],
            device_id=mate,
            device_id_type=MESH,
        )
        c.start()
        return c

    def hidden(q):
        i = q % 2
        acc[...] = jnp.zeros_like(acc)

        def one(k, _):
            columns = pl.ds(pl.multiple_of(k * 512, 512), 512)
            block = xs[q, :, columns]
            acc[0] += dot_t(block, gate_w[i, :, columns])
            acc[1] += dot_t(block, up_w[i, :, columns])
            return 0

        lax.fori_loop(0, 8, one, 0)
        columns = pl.ds(pl.multiple_of((tp // 2) * 384, 128), 384)
        gate = acc[0]
        hs[q, :, columns] = (gate / (1.0 + jnp.exp(-gate)) * acc[1]).astype(BF16)
        h_ring[q].start()

    def out(q):
        s, i = q // 2, q % 2

        def one(n, _):
            columns = pl.ds(pl.multiple_of(n * 256, 256), 256)
            mine = pl.ds(pl.multiple_of(core * 512 + n * 256, 256), 256)
            theirs = pl.ds(pl.multiple_of(512 - core * 512 + n * 256, 256), 256)
            block = hs[q]
            swap[s, i, :, columns] = dot(block, down_w[i, :, theirs]).astype(BF16)
            outs[s, 2 * core + i, :, columns] = dot(block, down_w[i, :, mine]).astype(BF16)
            return 0

        lax.fori_loop(0, 2, one, 0)
        c = pltpu.make_async_remote_copy(
            swap.at[s, i],
            outs.at[s, 2 * core + i],
            c_send.at[2 + q],
            c_recv.at[2 + q],
            device_id=mate,
            device_id_type=MESH,
        )
        c.start()
        return c

    def ungroup():
        def one(g, _):
            rows = pl.ds(pl.multiple_of(g * BLOCK, 16), BLOCK)
            for h in range(2):
                block = outs[0, :, rows, pl.ds(h * 256, 256)].reshape(ROWS, 256)
                outgoing[0, h, g] = dot(perm[...], block).astype(BF16).reshape(SIDE, BLOCK, 256)
            return 0

        lax.fori_loop(0, SIDE, one, 0)
        give[0].start(0)

    def ungroup_pair(i):
        def one(g, _):
            rows = pl.ds(pl.multiple_of(g * BLOCK, 16), BLOCK)
            for h in range(2):
                columns = pl.ds(h * 256, 256)
                total = dot(pair_perm[0], outs[1, i, rows, columns]) + dot(pair_perm[1], outs[1, 2 + i, rows, columns])
                out_pair[i, h, g] = total.astype(BF16).reshape(SIDE, PAIR, 256)
            return 0

        lax.fori_loop(0, SIDE, one, 0)
        give[1 + i].start(0)

    def choose():
        def one(d, _):
            x, z = d // SIDE, lax.rem(d, SIDE)
            home = home_s[spare_s[d]] // 4
            for h in range(2):
                chosen[h, x, z] = spread[h, home // SIDE, lax.rem(home, SIDE)]
            return 0

        lax.fori_loop(0, 16, one, 0)
        for d in range(1, SIDE):
            along_x, along_z = lax.rem(ex + d, SIDE) * SIDE + ez, ex * SIDE + lax.rem(ez + d, SIDE)
            pl.semaphore_signal(credit, inc=1, device_id=(along_x, tp), device_id_type=MESH)
            pl.semaphore_signal(credit, inc=1, device_id=(along_z, tp), device_id_type=MESH)
        pl.semaphore_wait(credit, 6)
        gather.start(0)

    def place(s):
        places, _ = slot_places(ids_ref[s], home_ref[...])

        def one(x, _):
            spread_rows, within = rows_of(x)
            placing = jnp.where(dot(spread_rows, places) == within, 1.0, 0.0).astype(BF16)
            for h in range(2):
                block = dot(placing, tok_ref[s, :, h * 256 : (h + 1) * 256]).astype(BF16)
                outgoing[s, h, x] = block.reshape(SIDE, BLOCK, 256)
            return 0

        lax.fori_loop(0, SIDE, one, 0)

    def fetch(j):
        h, two, b = j // 8, lax.rem(j, 8), lax.rem(j, 3)
        rows = pl.ds(pl.multiple_of(h * 96, 16), 96)
        columns = pl.ds(pl.multiple_of(two * 512, 512), 512)
        low = pl.ds(pl.multiple_of(h * 768 + two * 96, 16), 96)
        to = pl.ds(pl.multiple_of(b * 96, 16), 96)
        return [
            pltpu.make_async_copy(wg.at[:, rows, columns], hs.at[:, to, pl.ds(0, 512)], p_local.at[b, 0]),
            pltpu.make_async_copy(wu.at[:, rows, columns], hs.at[:, to, pl.ds(512, 512)], p_local.at[b, 1]),
            pltpu.make_async_copy(wd.at[:, low, :], hs.at[:, to, pl.ds(1024, 512)], p_local.at[b, 2]),
        ]

    def fetch_start(j):
        for c in fetch(j):
            c.start()

    def cut(first, end):
        def find(d, own):
            slot = home_s[spare_s[d]]
            return jnp.maximum(own, jnp.where(slot // 4 == ep, lax.rem(slot, 4), 0))

        own = lax.fori_loop(0, 16, find, jnp.int32(0))

        def one(j, _):
            for c in fetch(j):
                c.wait()
            h, two, b = j // 8, lax.rem(j, 8), lax.rem(j, 3)
            px, pair = two // 2, lax.rem(two, 2)

            def pick(low, rows, columns):
                at = pl.ds(pl.multiple_of(b * 96 + low, 16), rows)
                value = hs[0, at, columns]
                for k in range(1, 4):
                    value = jnp.where(own == k, hs[k, at, columns], value)
                return value

            for z in range(2):
                to = chosen.at[h, px, 2 * pair + z]
                for n in range(2):
                    to[pl.ds(96 * n, 96)] = pick(0, 96, pl.ds(512 * n + 256 * z, 256))
                    to[pl.ds(192 + 48 * n, 48)] = pick(48 * z, 48, pl.ds(1024 + 256 * n, 256))
            return 0

        def more(j, _):
            one(j, 0)
            fetch_start(j + 3)
            return 0

        lax.fori_loop(first, min(end, 13), more, 0)
        if end == 16:
            lax.fori_loop(13, 16, one, 0)

    for j in range(3):
        fetch_start(j)
    place(0)
    pl.semaphore_wait(barrier, 9)
    deal[0].start(0)
    for mine, theirs in weights:
        theirs.start()
        mine.start()
    deal[0].forward()
    place(1)
    deal[0].arrive(1)
    swap_x = [regroup(0)]
    deal[1].start(0)
    swap_x[0].wait()
    x_ring[0].start()
    cut(0, 8)
    deal[1].forward()
    cut(8, 16)
    scatter.start(0)
    x_ring[0].forward()
    x_ring[1].start()
    for mine, theirs in weights:
        mine.wait()
        theirs.wait_recv()
    x_ring[0].arrive()
    hidden(0)
    deal[1].arrive(1)
    swap_x.append(regroup(1))
    swap_x[1].wait()
    x_ring[1].forward()
    x_ring[2].start()
    h_ring[0].forward()
    scatter.forward()
    x_ring[1].arrive()
    hidden(1)
    h_ring[0].arrive()
    swap_o = [out(0)]
    x_ring[2].forward()
    x_ring[3].start()
    h_ring[1].forward()
    scatter.arrive(1)
    scatter.sent()
    choose()
    x_ring[2].arrive()
    hidden(2)
    h_ring[1].arrive()
    swap_o.append(out(1))
    swap_o[0].wait()
    swap_o[1].wait()
    for one in deal:
        one.sent()
    ungroup()
    x_ring[3].forward()
    h_ring[2].forward()
    gather.forward()
    x_ring[3].arrive()
    hidden(3)
    give[0].forward()
    h_ring[2].arrive()
    swap_o.append(out(2))
    swap_o[2].wait()
    ungroup_pair(0)
    h_ring[3].forward()
    h_ring[3].arrive()
    swap_o.append(out(3))
    swap_o[3].wait()
    ungroup_pair(1)
    give[1].forward()
    give[2].forward()
    gather.arrive(1)
    for one in give:
        one.arrive(1)
    for one in (*give, gather, *x_ring, *h_ring):
        one.sent()
    for _, theirs in weights:
        theirs.wait_send()


def permutation():
    index = np.arange(ROWS).reshape(SIDE, SIDE, CAP).transpose(1, 0, 2).reshape(-1)
    return np.eye(ROWS, dtype=np.float32)[index]


def pair_permutations():
    out = np.zeros((2, SIDE * PAIR, BLOCK), np.float32)
    for c in range(2):
        for z in range(SIDE):
            out[c, z * PAIR + c * CAP + np.arange(CAP), z * CAP + np.arange(CAP)] = 1.0
    return out


def shards(tokens, expert_ids, route_weight, gate_weight, up_weight, down_weight, home_slot, spare_expert):
    ids = expert_ids.transpose(0, 2, 1)
    home_row = home_slot.reshape(1, SLOTS)
    piece_shape = jax.ShapeDtypeStruct((2, SIDE, SIDE, PIECE, 256), BF16)
    row_shape = jax.ShapeDtypeStruct((STEPS, 2, SIDE, SIDE, BLOCK, 256), BF16)
    one_shape = jax.ShapeDtypeStruct((2, SIDE, SIDE, BLOCK, 256), BF16)
    pair_shape = jax.ShapeDtypeStruct((2, 2, SIDE, SIDE, PAIR, 256), BF16)

    returned, returned_pair, landed, *_ = pl.pallas_call(
        main_kernel,
        out_shape=(one_shape, pair_shape, piece_shape, piece_shape),
        in_specs=[SM, SM, VM, VM, VM, VM, VM, HBM, HBM, HBM],
        out_specs=(HBM,) * 4,
        scratch_shapes=[
            pltpu.VMEM((2, 384, 4096), BF16),
            pltpu.VMEM((2, 384, 4096), BF16),
            pltpu.VMEM((2, 1536, 1024), BF16),
            pltpu.VMEM((4, ROWS, 4096), BF16),
            pltpu.VMEM((4, ROWS, 1536), BF16),
            pltpu.VMEM((STEPS, 2, ROWS, 512), BF16),
            pltpu.VMEM((STEPS, 4, ROWS, 512), BF16),
            pltpu.VMEM(row_shape.shape, BF16),
            pltpu.VMEM(row_shape.shape, BF16),
            pltpu.VMEM(row_shape.shape, BF16),
            pltpu.VMEM(one_shape.shape, BF16),
            pltpu.VMEM(pair_shape.shape, BF16),
            pltpu.VMEM(pair_shape.shape, BF16),
            pltpu.VMEM(piece_shape.shape, BF16),
            pltpu.VMEM(piece_shape.shape, BF16),
            pltpu.VMEM((2, ROWS, 384), F32),
            pltpu.SemaphoreType.DMA((7, 2, 2, 4)),
            pltpu.SemaphoreType.DMA((7, 2, 2, 4)),
            pltpu.SemaphoreType.DMA((4, 4)),
            pltpu.SemaphoreType.DMA((4, 4)),
            pltpu.SemaphoreType.DMA((4, 4)),
            pltpu.SemaphoreType.DMA((4, 4)),
            pltpu.SemaphoreType.DMA((6,)),
            pltpu.SemaphoreType.DMA((6,)),
            pltpu.SemaphoreType.DMA((3,)),
            pltpu.SemaphoreType.DMA((3,)),
            pltpu.SemaphoreType.DMA((3,)),
            pltpu.SemaphoreType.DMA((3, 3)),
            pltpu.SemaphoreType.REGULAR,
        ],
        compiler_params=pltpu.CompilerParams(
            collective_id=0, has_side_effects=True, vmem_limit_bytes=60 * 2**20
        ),
        name="exchange",
    )(
        home_slot,
        spare_expert,
        home_row,
        ids,
        tokens,
        jnp.asarray(permutation(), BF16),
        jnp.asarray(pair_permutations(), BF16),
        gate_weight,
        up_weight,
        down_weight,
    )

    return pl.pallas_call(
        mix_kernel,
        out_shape=(
            jax.ShapeDtypeStruct(tokens.shape, BF16),
            jax.ShapeDtypeStruct((1,) + gate_weight.shape[1:], BF16),
            jax.ShapeDtypeStruct((1,) + up_weight.shape[1:], BF16),
            jax.ShapeDtypeStruct((1,) + down_weight.shape[1:], BF16),
        ),
        in_specs=[VM, VM, VM, HBM, HBM, HBM],
        out_specs=(VM, HBM, HBM, HBM),
        scratch_shapes=[
            pltpu.VMEM(one_shape.shape, BF16),
            pltpu.VMEM(pair_shape.shape, BF16),
            pltpu.VMEM(piece_shape.shape, BF16),
            pltpu.VMEM(gate_weight.shape[1:], BF16),
            pltpu.VMEM(up_weight.shape[1:], BF16),
            pltpu.VMEM(down_weight.shape[1:], BF16),
            pltpu.SemaphoreType.DMA((4,)),
            pltpu.SemaphoreType.DMA((2, 3)),
        ],
        compiler_params=pltpu.CompilerParams(vmem_limit_bytes=60 * 2**20),
        name="mix",
    )(ids, route_weight.transpose(0, 2, 1), home_row, returned, returned_pair, landed)


def solution(mesh):
    placed = (
        P(None, "ep", "tp"),
        P(None, "ep", None),
        P(None, "ep", None),
        P("ep", "tp", None),
        P("ep", "tp", None),
        P("ep", None, "tp"),
        P(),
        P(),
    )
    return jax.shard_map(
        shards,
        mesh=mesh,
        in_specs=placed,
        out_specs=(
            P(None, "ep", "tp"),
            P("ep", "tp", None),
            P("ep", "tp", None),
            P("ep", None, "tp"),
        ),
        check_vma=False,
    )
```
